32 devices in a mesh: chan: 4 (over y, x), win: 8 (over z, core).
Axes of the slice: x: 2, y: 2, z: 4, core: 2. Of those that a mesh axis runs over, the one named last changes fastest.
Arguments:
- traces: float32 [256, 16, 1024], P('chan', 'win'), may hold values from -80 to 80, as said below
- needed: int32 [4, 48], replicated, may hold values from 0 to 255, as said below
- home_slot: int32 [8, 8], P('chan'), may hold values from 0 to 47, as said below
- partner_slot: int32 [8, 16], P('chan'), may hold values from 0 to 47, as said below
- live_blocks: int32 [4], P('chan'), may hold values from 1 to 2, as said below
Outputs:
- correlations: float32 [1024, 1024], P(('chan', 'win'))
The draws below stay inside these ranges and needn't reach their ends.
Inputs may be any that keep to these rules, and one draw needn't show every extreme that they name: `traces`: samples are bounded by the range. `needed`: each row lists 48 distinct channels in increasing order; row d holds exactly 24 channels of its own group d * 64 .. (d + 1) * 64 - 1 and at most 24 of any other group of 64 channels. `home_slot`: within one block the 8 home positions and 16 partner positions are all distinct. `partner_slot`: within one block the 8 home positions and 16 partner positions are all distinct. `live_blocks`: some owner uses all 2 slots and another owner uses only one.
All inputs are finite; a program needn't handle non-finite values.
Results may differ from the reference program's by a relative error of at most 0.0041.
Values may be sent and summed in bfloat16 or wider, within the bound.
A program may use at most 64 MiB of HBM per device.

```python
import math
import jax
import jax.numpy as jnp
from jax import lax

NFFT = 1024
C_DEV = 64
BLK_OWN = 2
HOMES = 8
PARTNERS = 16
NEED = 48
CAP = 24
CHANNELS = 256
WINDOWS = 16
PAIRS = 1024
N_CHAN = 4


def draw_traces(key, part):
    draw_keys = jax.random.split(key, 5)
    full_shape = (CHANNELS, WINDOWS, NFFT)
    row_shape = (CHANNELS, WINDOWS, 1)
    noise_part = jnp.clip(jax.random.normal(draw_keys[0], full_shape, jnp.float32), -4.0, 4.0)
    gain_rows = jnp.exp(jax.random.uniform(draw_keys[1], row_shape, jnp.float32, math.log(0.5), math.log(5.0)))
    peak_bins = jax.random.randint(draw_keys[2], row_shape, 1, NFFT // 2)
    peak_phase = jax.random.uniform(draw_keys[3], row_shape, jnp.float32, -math.pi, math.pi)
    height = jax.random.uniform(draw_keys[4], row_shape, jnp.float32, 0.0, 3.0)
    sample_index = jnp.arange(NFFT, dtype=jnp.int32)
    peak_angle = (peak_bins * sample_index % NFFT).astype(jnp.float32) * (2.0 * math.pi / NFFT) + peak_phase
    return gain_rows * (noise_part + height * jnp.cos(peak_angle))


def draw_needed(key, part):
    tokens = N_CHAN * CAP
    token_group = jnp.arange(tokens, dtype=jnp.int32) // CAP
    token_rank = jnp.arange(tokens, dtype=jnp.int32) % CAP
    order_keys = jax.random.split(jax.random.fold_in(key, 11), N_CHAN)
    row_keys = jax.random.split(jax.random.fold_in(key, 12), N_CHAN)
    shuffles = jax.vmap(lambda row_key: jax.random.permutation(row_key, C_DEV))(row_keys)[:, :CAP].astype(jnp.int32)

    def one_owner(owner_key, owner_index):
        shuffled = jax.random.permutation(owner_key, tokens).astype(jnp.int32)
        priority = jnp.where(token_group == owner_index, shuffled - tokens, shuffled)
        chosen = jnp.argsort(priority, stable=True)[:NEED]
        chosen_group = token_group[chosen]
        channel = chosen_group * C_DEV + shuffles[chosen_group, token_rank[chosen]]
        return jnp.sort(channel)
    return jax.vmap(one_owner)(order_keys, jnp.arange(N_CHAN, dtype=jnp.int32)).astype(jnp.int32)


def block_slots(key):
    block_keys = jax.random.split(jax.random.fold_in(key, 21), N_CHAN * BLK_OWN)
    return jax.vmap(lambda block_key: jax.random.permutation(block_key, NEED)[:HOMES + PARTNERS])(block_keys).astype(jnp.int32)


def draw_home_slot(key, part):
    return block_slots(key)[:, :HOMES]


def draw_partner_slot(key, part):
    return block_slots(key)[:, HOMES:]


def draw_live_blocks(key, part):
    counts = jax.random.randint(jax.random.fold_in(key, 31), (N_CHAN,), 1, BLK_OWN + 1)
    fullest = jax.random.randint(jax.random.fold_in(key, 32), (), 0, N_CHAN)
    step_away = jax.random.randint(jax.random.fold_in(key, 33), (), 1, N_CHAN)
    sparsest = (fullest + step_away) % N_CHAN
    owner_index = jnp.arange(N_CHAN, dtype=jnp.int32)
    counts = jnp.where(owner_index == sparsest, 1, counts)
    return jnp.where(owner_index == fullest, BLK_OWN, counts).astype(jnp.int32)


def setup_inputs(seed: int = 0) -> dict:
    seeds = jax.random.split(jax.random.key(seed), 6)
    traces = draw_traces(jax.random.fold_in(seeds[5], 71), 0)
    needed = draw_needed(jax.random.fold_in(seeds[5], 71), 0)
    home_slot = draw_home_slot(jax.random.fold_in(seeds[5], 71), 0)
    partner_slot = draw_partner_slot(jax.random.fold_in(seeds[5], 71), 0)
    live_blocks = draw_live_blocks(jax.random.fold_in(seeds[5], 71), 0)
    return {"traces": traces, "needed": needed, "home_slot": home_slot, "partner_slot": partner_slot, "live_blocks": live_blocks}


band_reach = 64

def forward_table(samples):
    freq_bins = samples // 2
    sample_index = jnp.arange(samples, dtype=jnp.int32)[:, None]
    freq_index = jnp.arange(freq_bins, dtype=jnp.int32)[None, :]
    phase_angle = (sample_index * freq_index % samples).astype(jnp.float32) * (2.0 * math.pi / samples)
    return jnp.concatenate([jnp.cos(phase_angle), -jnp.sin(phase_angle)], axis=1)

def inverse_table(samples):
    freq_bins = samples // 2
    freq_index = jnp.arange(freq_bins, dtype=jnp.int32)[:, None]
    lag_shift = (jnp.arange(samples, dtype=jnp.int32) - samples // 2) % samples
    phase_angle = (freq_index * lag_shift[None, :] % samples).astype(jnp.float32) * (2.0 * math.pi / samples)
    weight = jnp.where(freq_index == 0, 1.0, 2.0).astype(jnp.float32)
    return jnp.concatenate([weight * jnp.cos(phase_angle), -weight * jnp.sin(phase_angle)], axis=0)

def band_table(freq_bins):
    bin_index = jnp.arange(freq_bins, dtype=jnp.int32)
    inside = (jnp.abs(bin_index[:, None] - bin_index[None, :]) <= band_reach).astype(jnp.float32)
    return inside / lax.optimization_barrier(jnp.sum(inside, axis=0, keepdims=True))

def whiten(trace_rows):
    samples = trace_rows.shape[-1]
    freq_bins = samples // 2
    spectrum = jnp.dot(trace_rows, forward_table(samples), precision=lax.Precision.HIGHEST)
    power_bins = spectrum[:, :freq_bins] ** 2 + spectrum[:, freq_bins:] ** 2
    smooth = jnp.dot(power_bins, band_table(freq_bins), precision=lax.Precision.HIGHEST)
    factor = 1.0 / jnp.sqrt(smooth + 1e-05)
    return (spectrum * jnp.concatenate([factor, factor], axis=1)).astype(jnp.bfloat16)

def cross_spectra(home_spectra, partners):
    freq_bins = home_spectra.shape[-1] // 2
    home_f = home_spectra.astype(jnp.float32)
    part_f = partners.astype(jnp.float32)

    def product(left_side, right_side):
        return jnp.einsum('bhwf,bpwf->bhpf', left_side, right_side, precision=lax.Precision.HIGHEST)
    home_re, home_im = (home_f[..., :freq_bins], home_f[..., freq_bins:])
    part_re, part_im = (part_f[..., :freq_bins], part_f[..., freq_bins:])
    real_part = product(home_re, part_re) + product(home_im, part_im)
    imag_part = product(home_im, part_re) - product(home_re, part_im)
    joined = jnp.concatenate([real_part, imag_part], axis=-1)
    return joined.reshape(-1, joined.shape[-1])

def reference(traces, needed, home_slot, partner_slot, live_blocks):
    groups = traces.reshape(N_CHAN, C_DEV * WINDOWS, NFFT)
    whitened = lax.map(whiten, groups).reshape(CHANNELS, WINDOWS, NFFT)
    inverse = inverse_table(NFFT)
    norm_scale = 1.0 / math.sqrt(NFFT * WINDOWS)
    homes_all = home_slot.reshape(N_CHAN, BLK_OWN, HOMES)
    partners_all = partner_slot.reshape(N_CHAN, BLK_OWN, PARTNERS)
    block_index = jnp.arange(BLK_OWN * HOMES * PARTNERS, dtype=jnp.int32) // (HOMES * PARTNERS)

    def one_owner(packed):
        listed, home_rows, partner_rows, live_count = packed
        table_rows = whitened[listed]
        cross_terms = cross_spectra(table_rows[home_rows], table_rows[partner_rows])
        correlated = jnp.dot(cross_terms, inverse, precision=lax.Precision.HIGHEST) * norm_scale
        live_mask = (block_index < live_count).astype(jnp.float32)
        return correlated * live_mask[:, None]
    stacked = lax.map(one_owner, (needed, homes_all, partners_all, live_blocks))
    return stacked.reshape(PAIRS, NFFT)
```

```python
import functools
import math

import jax
import jax.numpy as jnp
import ml_dtypes
import numpy as np
from jax import lax
from jax.experimental import pallas as pl
from jax.experimental.pallas import tpu as pltpu
from jax.sharding import PartitionSpec as P

MESH = pl.DeviceIdType.MESH
BAND_REACH = 64
CHUNKS = 4


def split_table(table):
    high = table.astype(np.float32).astype(ml_dtypes.bfloat16)
    low = (table - high.astype(np.float64)).astype(np.float32).astype(ml_dtypes.bfloat16)
    return high, low


@functools.lru_cache(maxsize=None)
def tables(samples):
    quarter, half = samples // 4, samples // 2
    eighth = samples // 8
    bins_a = np.arange(0, half, 4)
    bins_b = np.arange(2, half, 4)
    bins_o = np.arange(1, half, 2)

    def forward(length, bins):
        phase = (np.arange(length)[:, None] * bins[None, :] % samples) * (2.0 * np.pi / samples)
        return np.cos(phase), -np.sin(phase)

    def inverse(length, bins):
        phase = (bins[:, None] * np.arange(length)[None, :] % samples) * (2.0 * np.pi / samples)
        weight = np.where(bins == 0, 1.0, 2.0)[:, None]
        return weight * np.cos(phase), -weight * np.sin(phase)

    odd_cos, odd_sin = forward(half, bins_o)
    fwd_a = np.concatenate(forward(quarter, bins_a), axis=1)
    fwd_b = np.concatenate(forward(quarter, bins_b), axis=1)
    fwd_o = np.concatenate(
        [odd_cos[:, :eighth], odd_sin[:, :eighth], odd_cos[:, eighth:], odd_sin[:, eighth:]], axis=1
    )
    fwd_even = np.stack([x for t in (fwd_a, fwd_b) for x in split_table(t)])
    fwd_odd = np.stack(split_table(fwd_o))
    order = np.concatenate([bins_a, bins_b, bins_o])
    inside = np.abs(order[:, None] - order[None, :]) <= BAND_REACH
    band = inside.astype(np.float32).astype(ml_dtypes.bfloat16)
    share = (1.0 / inside.sum(axis=0, keepdims=True)).astype(np.float32)
    inv_cos, inv_sin = inverse(half, bins_o)
    inv_even = np.stack(
        [
            split_table(np.concatenate(inverse(quarter, bins), axis=0))[0]
            for bins in (bins_a, bins_b)
        ]
    )
    inv_odd = np.stack(
        [
            split_table(np.concatenate([inv_cos[rows], inv_sin[rows]], axis=0))[0]
            for rows in (slice(0, eighth), slice(eighth, None))
        ]
    )
    return fwd_even, fwd_odd, band, share, inv_even, inv_odd


def dot(left, right):
    return jnp.dot(left, right, preferred_element_type=jnp.float32)


def halves(value):
    high = value.astype(jnp.bfloat16)
    low = (value - high.astype(jnp.float32)).astype(jnp.bfloat16)
    return high, low


def as_column(row):
    n = row.shape[1]
    eye = lax.broadcasted_iota(jnp.int32, (n, n), 0) == lax.broadcasted_iota(jnp.int32, (n, n), 1)
    return jnp.sum(jnp.where(eye, jnp.broadcast_to(row, (n, n)), 0), axis=1, keepdims=True)


def kernel(
    dims,
    traces_hbm,
    needed_ref,
    home_ref,
    partner_ref,
    live_ref,
    fwd_even_hbm,
    fwd_odd_hbm,
    band_hbm,
    share_ref,
    inv_even_hbm,
    inv_odd_hbm,
    out_ref,
    traces,
    fwd_even,
    fwd_odd,
    band,
    inv_even,
    inv_odd,
    listed_out,
    listed_in,
    terms,
    terms_out,
    pair_in,
    chip_sum,
    chip_out,
    chip_in,
    load_sem,
    list_send,
    list_recv,
    pair_send,
    pair_recv,
    chip_send,
    chip_recv,
):
    groups, win_count, chan_dev, win_dev, samples, listing, cap, cap_rows, blocks, homes, partners = dims
    chips = win_count // 2
    pairs = blocks * homes * partners
    share_rows = pairs // win_count
    pad_rows = terms.shape[2] // chips
    quarter, half, eighth = samples // 4, samples // 2, samples // 8
    group = lax.axis_index("chan")
    win = lax.axis_index("win")
    chip, core = win // 2, win % 2

    loads = [
        pltpu.make_async_copy(src, dst, load_sem.at[i])
        for i, (src, dst) in enumerate(
            (
                (traces_hbm, traces),
                (fwd_even_hbm, fwd_even),
                (fwd_odd_hbm, fwd_odd),
                (band_hbm, band),
                (inv_even_hbm, inv_even),
                (inv_odd_hbm, inv_odd),
            )
        )
    ]
    for load in loads:
        load.start()

    barrier = pltpu.get_barrier_semaphore()
    group_peers = [lax.rem(group + d, groups) for d in range(1, groups)]
    chip_peers = [lax.rem(chip + d, chips) for d in range(1, chips)]
    for peer in group_peers:
        pl.semaphore_signal(barrier, inc=1, device_id={"chan": peer}, device_id_type=MESH)
    pl.semaphore_signal(
        barrier, inc=1, device_id={"win": chip * 2 + 1 - core}, device_id_type=MESH
    )
    for peer in chip_peers:
        pl.semaphore_signal(
            barrier, inc=1, device_id={"win": peer * 2 + core}, device_id_type=MESH
        )

    lanes = win_dev * chan_dev
    lane = lax.broadcasted_iota(jnp.int32, (1, lanes), 1)
    lane_win = sum([(lane >= w * chan_dev).astype(jnp.int32) for w in range(1, win_dev)])
    lane_chan = lane - lane_win * chan_dev
    first_mine = group * chan_dev
    place = lax.broadcasted_iota(jnp.int32, (listing, lanes), 0)
    out_row = lax.broadcasted_iota(jnp.int32, (cap_rows, lanes), 0)
    choose = []
    for d in range(groups):
        owner = lax.rem(group + d, groups)
        column = as_column(needed_ref[pl.ds(owner, 1), :])
        hit = column == (lane_chan + first_mine)
        found = jnp.sum(jnp.where(hit, place + 1, 0), axis=0, keepdims=True)
        begin = jnp.sum((column < first_mine).astype(jnp.int32), axis=0, keepdims=True)
        target = jnp.where(found > 0, found - 1 - begin + lane_win * cap, -1)
        choose.append(jnp.where(out_row == target, 1.0, 0.0))
    choose = jnp.concatenate(choose, axis=0).astype(jnp.bfloat16)

    mine = needed_ref[pl.ds(group, 1), :]
    arrived = lax.broadcasted_iota(jnp.int32, (1, groups * cap_rows), 1)
    code = jnp.full((1, groups * cap_rows), -1, jnp.int32)
    for d in range(groups):
        source = lax.rem(group + groups - d, groups)
        begin = jnp.sum(
            (mine < source * chan_dev).astype(jnp.int32), axis=1, keepdims=True
        )
        for w in range(win_dev):
            low = d * cap_rows + w * cap
            within = (arrived >= low) & (arrived < low + cap)
            code = jnp.where(within, arrived - low + begin + w * listing, code)
    wanted = [as_column(partner_ref[b : b + 1, :]) for b in range(blocks)]
    wanted += [as_column(home_ref[b : b + 1, :]) for b in range(blocks)]
    wanted = jnp.concatenate(wanted, axis=0)
    per_win = blocks * (homes + partners)
    wanted = jnp.concatenate([wanted + w * listing for w in range(win_dev)], axis=0)
    pick = jnp.where(wanted == code, 1.0, 0.0).astype(jnp.bfloat16)

    loads[0].wait()
    rows = jnp.concatenate([traces[:, w, :] for w in range(win_dev)], axis=0)
    count = rows.shape[0]
    folded = rows[:, :half] + rows[:, half:]
    odd_in = rows[:, :half] - rows[:, half:]
    even_in = (folded[:, :quarter] + folded[:, quarter:], folded[:, :quarter] - folded[:, quarter:])

    def transform(value, high_table, low_table):
        high, low = halves(value)
        both = dot(jnp.concatenate([high, low], axis=0), high_table)
        return both[:count] + both[count:] + dot(high, low_table)

    loads[1].wait()
    spectra = [
        transform(even_in[0], fwd_even[0], fwd_even[1]),
        transform(even_in[1], fwd_even[2], fwd_even[3]),
    ]
    loads[2].wait()
    odd_out = transform(odd_in, fwd_odd[0], fwd_odd[1])
    spectra += [odd_out[:, :quarter], odd_out[:, quarter:]]
    power = jnp.concatenate([s[:, :eighth] ** 2 + s[:, eighth:] ** 2 for s in spectra], axis=1)
    loads[3].wait()
    both = dot(jnp.concatenate(halves(power), axis=0), band[...])
    smooth = (both[:count] + both[count:]) * share_ref[...]
    factor = 1.0 / jnp.sqrt(smooth + 1e-05)

    pl.semaphore_wait(barrier, (groups - 1) + 1 + (chips - 1))

    list_copies = []
    for k in range(CHUNKS):
        scale = factor[:, k * eighth : (k + 1) * eighth]
        whitened = jnp.concatenate(
            [spectra[k][:, :eighth] * scale, spectra[k][:, eighth:] * scale], axis=1
        ).astype(jnp.bfloat16)
        chosen = dot(choose, whitened).astype(jnp.bfloat16)
        listed_in[k, 0] = chosen[:cap_rows]
        copies = []
        for d in range(1, groups):
            listed_out[k, d - 1] = chosen[d * cap_rows : (d + 1) * cap_rows]
            copies.append(
                pltpu.make_async_remote_copy(
                    src_ref=listed_out.at[k, d - 1],
                    dst_ref=listed_in.at[k, d],
                    send_sem=list_send.at[k, d - 1],
                    recv_sem=list_recv.at[k, d - 1],
                    device_id={"chan": group_peers[d - 1]},
                    device_id_type=MESH,
                )
            )
            copies[-1].start()
        list_copies.append(copies)

    pair_copies = [
        pltpu.make_async_remote_copy(
            src_ref=terms_out.at[k, 1 - core],
            dst_ref=pair_in.at[k],
            send_sem=pair_send.at[k],
            recv_sem=pair_recv.at[k],
            device_id={"win": chip * 2 + 1 - core},
            device_id_type=MESH,
        )
        for k in range(CHUNKS)
    ]
    chip_copies = [
        [
            pltpu.make_async_remote_copy(
                src_ref=chip_out.at[k, chip_peers[d - 1]],
                dst_ref=chip_in.at[k, d - 1],
                send_sem=chip_send.at[k, d - 1],
                recv_sem=chip_recv.at[k, d - 1],
                device_id={"win": chip_peers[d - 1] * 2 + core},
                device_id_type=MESH,
            )
            for d in range(1, chips)
        ]
        for k in range(CHUNKS)
    ]

    def cross(k):
        for copy in list_copies[k]:
            copy.wait_recv()
        table = dot(pick, listed_in[k].reshape(groups * cap_rows, quarter))
        piece = min(partners, share_rows)
        for b in range(blocks):
            for i in range(homes):
                real = imag = None
                for w in range(win_dev):
                    at = w * per_win + blocks * partners + b * homes + i
                    home_re = table[at : at + 1, :eighth]
                    home_im = table[at : at + 1, eighth:]
                    at = w * per_win + b * partners
                    part_re = table[at : at + partners, :eighth]
                    part_im = table[at : at + partners, eighth:]
                    add_re = home_re * part_re + home_im * part_im
                    add_im = home_im * part_re - home_re * part_im
                    real = add_re if real is None else real + add_re
                    imag = add_im if imag is None else imag + add_im
                term = jnp.concatenate([real, imag], axis=1)
                for j in range(0, partners, piece):
                    row = (b * homes + i) * partners + j
                    owner, inner = row // share_rows, row % share_rows
                    at = (owner // 2) * pad_rows + inner
                    terms[k, owner % 2, at : at + piece, :] = term[j : j + piece]
        terms_out[k, 1 - core] = terms[k, 1 - core].astype(jnp.bfloat16)
        pair_copies[k].start()

    def across(k):
        pair_copies[k].wait_recv()
        total = terms[k, core] + pair_in[k].astype(jnp.float32)
        total = total.reshape(chips, pad_rows, quarter)
        chip_sum[k] = total
        chip_out[k] = total.astype(jnp.bfloat16)
        for copy in chip_copies[k]:
            copy.start()

    for k in range(CHUNKS):
        cross(k)
        if k:
            across(k - 1)
    across(CHUNKS - 1)

    loads[4].wait()
    loads[5].wait()
    parts = []
    for k in range(CHUNKS):
        for copy in chip_copies[k]:
            copy.wait_recv()
        total = chip_sum[k, chip]
        for d in range(1, chips):
            total = total + chip_in[k, d - 1].astype(jnp.float32)
        table = inv_even[k] if k < 2 else inv_odd[k - 2]
        both = dot(jnp.concatenate(halves(total), axis=0), table)
        parts.append(both[:pad_rows] + both[pad_rows:])
    even = jnp.concatenate([parts[0] + parts[1], parts[0] - parts[1]], axis=1)
    odd = parts[2] + parts[3]
    norm = 1.0 / math.sqrt(samples * win_dev * win_count)
    row = win * share_rows + lax.broadcasted_iota(jnp.int32, (pad_rows, 1), 0)
    block = sum([(row >= b * homes * partners).astype(jnp.int32) for b in range(1, blocks)])
    gain = jnp.where(block < live_ref[0], norm, 0.0)
    out_ref[:, :half] = ((even - odd) * gain)[:share_rows]
    out_ref[:, half:] = ((even + odd) * gain)[:share_rows]

    for k in range(CHUNKS):
        for copy in list_copies[k] + [pair_copies[k]] + chip_copies[k]:
            copy.wait_send()


def body(traces, needed, home_slot, partner_slot, live_blocks):
    chan_dev, win_dev, samples = traces.shape
    groups, win_count = lax.axis_size("chan"), lax.axis_size("win")
    listing = needed.shape[1]
    cap = 2 * listing // groups
    cap_rows = -(-win_dev * cap // 16) * 16
    blocks, homes = home_slot.shape
    partners = partner_slot.shape[1]
    chips = win_count // 2
    share_rows = blocks * homes * partners // win_count
    pad_rows = max(share_rows, 16)
    quarter = samples // 4
    fwd_even, fwd_odd, band, share, inv_even, inv_odd = tables(samples)
    dims = (groups, win_count, chan_dev, win_dev, samples, listing, cap, cap_rows, blocks, homes, partners)
    vmem = pl.BlockSpec(memory_space=pltpu.VMEM)
    smem = pl.BlockSpec(memory_space=pltpu.SMEM)
    hbm = pl.BlockSpec(memory_space=pl.ANY)
    bf16, f32 = jnp.bfloat16, jnp.float32
    return pl.pallas_call(
        functools.partial(kernel, dims),
        out_shape=jax.ShapeDtypeStruct((share_rows, samples), f32),
        in_specs=[hbm, vmem, vmem, vmem, smem, hbm, hbm, hbm, vmem, hbm, hbm],
        out_specs=vmem,
        scratch_shapes=[
            pltpu.VMEM(traces.shape, f32),
            pltpu.VMEM(fwd_even.shape, bf16),
            pltpu.VMEM(fwd_odd.shape, bf16),
            pltpu.VMEM(band.shape, bf16),
            pltpu.VMEM(inv_even.shape, bf16),
            pltpu.VMEM(inv_odd.shape, bf16),
            pltpu.VMEM((CHUNKS, groups - 1, cap_rows, quarter), bf16),
            pltpu.VMEM((CHUNKS, groups, cap_rows, quarter), bf16),
            pltpu.VMEM((CHUNKS, 2, chips * pad_rows, quarter), f32),
            pltpu.VMEM((CHUNKS, 2, chips * pad_rows, quarter), bf16),
            pltpu.VMEM((CHUNKS, chips * pad_rows, quarter), bf16),
            pltpu.VMEM((CHUNKS, chips, pad_rows, quarter), f32),
            pltpu.VMEM((CHUNKS, chips, pad_rows, quarter), bf16),
            pltpu.VMEM((CHUNKS, chips - 1, pad_rows, quarter), bf16),
            pltpu.SemaphoreType.DMA((6,)),
            pltpu.SemaphoreType.DMA((CHUNKS, groups - 1)),
            pltpu.SemaphoreType.DMA((CHUNKS, groups - 1)),
            pltpu.SemaphoreType.DMA((CHUNKS,)),
            pltpu.SemaphoreType.DMA((CHUNKS,)),
            pltpu.SemaphoreType.DMA((CHUNKS, chips - 1)),
            pltpu.SemaphoreType.DMA((CHUNKS, chips - 1)),
        ],
        compiler_params=pltpu.CompilerParams(
            collective_id=0, has_side_effects=True, vmem_limit_bytes=40 * 1024 * 1024
        ),
        cost_estimate=pl.CostEstimate(
            flops=2_000_000_000, bytes_accessed=4_000_000, transcendentals=100_000
        ),
        name="whiten_cross_stack",
    )(
        traces,
        needed,
        home_slot,
        partner_slot,
        live_blocks,
        jnp.asarray(fwd_even),
        jnp.asarray(fwd_odd),
        jnp.asarray(band),
        jnp.asarray(share),
        jnp.asarray(inv_even),
        jnp.asarray(inv_odd),
    )


def solution(mesh):
    placed = (P("chan", "win", None), P(), P("chan", None), P("chan", None), P("chan"))
    return jax.shard_map(
        body, mesh=mesh, in_specs=placed, out_specs=P(("chan", "win"), None), check_vma=False
    )
```

```python
import functools
import math

import jax
import jax.numpy as jnp
import ml_dtypes
import numpy as np
from jax import lax
from jax.experimental import pallas as pl
from jax.experimental.pallas import tpu as pltpu
from jax.sharding import PartitionSpec as P

MESH = pl.DeviceIdType.MESH
BAND_REACH = 64
CHUNKS = 4


def split_table(table):
    high = table.astype(np.float32).astype(ml_dtypes.bfloat16)
    low = (table - high.astype(np.float64)).astype(np.float32).astype(ml_dtypes.bfloat16)
    return high, low


@functools.lru_cache(maxsize=None)
def tables(samples):
    quarter, half = samples // 4, samples // 2
    eighth = samples // 8
    bins_a = np.arange(0, half, 4)
    bins_b = np.arange(2, half, 4)
    bins_o = np.arange(1, half, 2)

    def forward(length, bins):
        phase = (np.arange(length)[:, None] * bins[None, :] % samples) * (2.0 * np.pi / samples)
        return np.cos(phase), -np.sin(phase)

    def inverse(length, bins):
        phase = (bins[:, None] * np.arange(length)[None, :] % samples) * (2.0 * np.pi / samples)
        weight = np.where(bins == 0, 1.0, 2.0)[:, None]
        return weight * np.cos(phase), -weight * np.sin(phase)

    odd_cos, odd_sin = forward(half, bins_o)
    fwd_a = np.concatenate(forward(quarter, bins_a), axis=1)
    fwd_b = np.concatenate(forward(quarter, bins_b), axis=1)
    fwd_o = np.concatenate(
        [odd_cos[:, :eighth], odd_sin[:, :eighth], odd_cos[:, eighth:], odd_sin[:, eighth:]], axis=1
    )
    fwd_even = np.stack([x for t in (fwd_a, fwd_b) for x in split_table(t)])
    fwd_odd = np.stack(split_table(fwd_o))
    order = np.concatenate([bins_a, bins_b, bins_o])
    inside = np.abs(order[:, None] - order[None, :]) <= BAND_REACH
    band = inside.astype(np.float32).astype(ml_dtypes.bfloat16)
    inv_cos, inv_sin = inverse(half, bins_o)
    inv_even = np.stack(
        [
            split_table(np.concatenate(inverse(quarter, bins), axis=0))[0]
            for bins in (bins_a, bins_b)
        ]
    )
    inv_odd = np.stack(
        [
            split_table(np.concatenate([inv_cos[rows], inv_sin[rows]], axis=0))[0]
            for rows in (slice(0, eighth), slice(eighth, None))
        ]
    )
    return fwd_even, fwd_odd, band, inv_even, inv_odd


def dot(left, right):
    return jnp.dot(left, right, preferred_element_type=jnp.float32)


def halves(value):
    high = value.astype(jnp.bfloat16)
    low = (value - high.astype(jnp.float32)).astype(jnp.bfloat16)
    return high, low


def as_column(row):
    n = row.shape[1]
    eye = lax.broadcasted_iota(jnp.int32, (n, n), 0) == lax.broadcasted_iota(jnp.int32, (n, n), 1)
    return jnp.sum(jnp.where(eye, jnp.broadcast_to(row, (n, n)), 0), axis=1, keepdims=True)


def kernel(
    dims,
    traces_hbm,
    needed_hbm,
    home_hbm,
    partner_hbm,
    live_hbm,
    fwd_even_hbm,
    fwd_odd_hbm,
    band_hbm,
    inv_even_hbm,
    inv_odd_hbm,
    out_ref,
    needed_ref,
    home_ref,
    partner_ref,
    live_ref,
    traces,
    fwd_even,
    fwd_odd,
    band,
    inv_even,
    inv_odd,
    listed_out,
    listed_in,
    terms,
    terms_out,
    pair_in,
    chip_sum,
    chip_out,
    chip_in,
    load_sem,
    list_send,
    list_recv,
    pair_send,
    pair_recv,
    chip_send,
    chip_recv,
):
    groups, win_count, chan_dev, win_dev, samples, listing, cap, cap_rows, blocks, homes, partners = dims
    chips = win_count // 2
    pairs = blocks * homes * partners
    share_rows = pairs // win_count
    pad_rows = terms.shape[2] // chips
    quarter, half, eighth = samples // 4, samples // 2, samples // 8
    group = lax.axis_index("chan")
    win = lax.axis_index("win")
    chip, core = win // 2, win % 2

    loads = [
        pltpu.make_async_copy(src, dst, load_sem.at[i])
        for i, (src, dst) in enumerate(
            (
                (traces_hbm, traces),
                (fwd_even_hbm, fwd_even),
                (fwd_odd_hbm, fwd_odd),
                (band_hbm, band),
                (inv_even_hbm, inv_even),
                (inv_odd_hbm, inv_odd),
                (needed_hbm, needed_ref),
                (home_hbm, home_ref),
                (partner_hbm, partner_ref),
                (live_hbm, live_ref),
            )
        )
    ]
    for i in (6, 7, 8, 0, 1, 2, 3, 4, 5, 9):
        loads[i].start()

    barrier = pltpu.get_barrier_semaphore()
    group_peers = [lax.rem(group + d, groups) for d in range(1, groups)]
    chip_peers = [lax.rem(chip + d, chips) for d in range(1, chips)]
    for peer in group_peers:
        pl.semaphore_signal(barrier, inc=1, device_id={"chan": peer}, device_id_type=MESH)
    pl.semaphore_signal(
        barrier, inc=1, device_id={"win": chip * 2 + 1 - core}, device_id_type=MESH
    )
    for peer in chip_peers:
        pl.semaphore_signal(
            barrier, inc=1, device_id={"win": peer * 2 + core}, device_id_type=MESH
        )

    lanes = win_dev * chan_dev
    lane = lax.broadcasted_iota(jnp.int32, (1, lanes), 1)
    lane_win = sum([(lane >= w * chan_dev).astype(jnp.int32) for w in range(1, win_dev)])
    lane_chan = lane - lane_win * chan_dev
    first_mine = group * chan_dev
    place = lax.broadcasted_iota(jnp.int32, (listing, lanes), 0)
    out_row = lax.broadcasted_iota(jnp.int32, (cap_rows, lanes), 0)
    for i in (6, 7, 8):
        loads[i].wait()
    choose = []
    for d in range(groups):
        owner = lax.rem(group + d, groups)
        column = as_column(needed_ref[pl.ds(owner, 1), :])
        hit = column == (lane_chan + first_mine)
        found = jnp.sum(jnp.where(hit, place + 1, 0), axis=0, keepdims=True)
        begin = jnp.sum((column < first_mine).astype(jnp.int32), axis=0, keepdims=True)
        target = jnp.where(found > 0, found - 1 - begin + lane_win * cap, -1)
        choose.append(jnp.where(out_row == target, 1.0, 0.0))
    choose = jnp.concatenate(choose, axis=0).astype(jnp.bfloat16)

    mine = needed_ref[pl.ds(group, 1), :]
    arrived = lax.broadcasted_iota(jnp.int32, (1, groups * cap_rows), 1)
    code = jnp.full((1, groups * cap_rows), -1, jnp.int32)
    for d in range(groups):
        source = lax.rem(group + groups - d, groups)
        begin = jnp.sum(
            (mine < source * chan_dev).astype(jnp.int32), axis=1, keepdims=True
        )
        for w in range(win_dev):
            low = d * cap_rows + w * cap
            within = (arrived >= low) & (arrived < low + cap)
            code = jnp.where(within, arrived - low + begin + w * listing, code)
    wanted = [as_column(partner_ref[b : b + 1, :]) for b in range(blocks)]
    wanted += [as_column(home_ref[b : b + 1, :]) for b in range(blocks)]
    wanted = jnp.concatenate(wanted, axis=0)
    per_win = blocks * (homes + partners)
    wanted = jnp.concatenate([wanted + w * listing for w in range(win_dev)], axis=0)
    pick = jnp.where(wanted == code, 1.0, 0.0).astype(jnp.bfloat16)

    loads[0].wait()
    rows = jnp.concatenate([traces[:, w, :] for w in range(win_dev)], axis=0)
    count = rows.shape[0]
    folded = rows[:, :half] + rows[:, half:]
    odd_in = rows[:, :half] - rows[:, half:]
    even_in = (folded[:, :quarter] + folded[:, quarter:], folded[:, :quarter] - folded[:, quarter:])

    def transform(value, high_table, low_table):
        high, low = halves(value)
        both = dot(jnp.concatenate([high, low], axis=0), high_table)
        return both[:count] + both[count:] + dot(high, low_table)

    loads[1].wait()
    spectra = [
        transform(even_in[0], fwd_even[0], fwd_even[1]),
        transform(even_in[1], fwd_even[2], fwd_even[3]),
    ]
    loads[2].wait()
    odd_out = transform(odd_in, fwd_odd[0], fwd_odd[1])
    spectra += [odd_out[:, :quarter], odd_out[:, quarter:]]
    power = jnp.concatenate([s[:, :eighth] ** 2 + s[:, eighth:] ** 2 for s in spectra], axis=1)
    loads[3].wait()
    both = dot(jnp.concatenate(halves(power), axis=0), band[...])
    spot = lax.broadcasted_iota(jnp.int32, (1, half), 1)
    bins = jnp.where(
        spot < eighth,
        spot * 4,
        jnp.where(spot < quarter, (spot - eighth) * 4 + 2, (spot - quarter) * 2 + 1),
    )
    members = jnp.minimum(bins + BAND_REACH, half - 1) - jnp.maximum(bins - BAND_REACH, 0) + 1
    smooth = (both[:count] + both[count:]) * (1.0 / members.astype(jnp.float32))
    factor = 1.0 / jnp.sqrt(smooth + 1e-05)

    pl.semaphore_wait(barrier, (groups - 1) + 1 + (chips - 1))

    list_copies = []
    for k in range(CHUNKS):
        scale = factor[:, k * eighth : (k + 1) * eighth]
        whitened = jnp.concatenate(
            [spectra[k][:, :eighth] * scale, spectra[k][:, eighth:] * scale], axis=1
        ).astype(jnp.bfloat16)
        chosen = dot(choose, whitened).astype(jnp.bfloat16)
        listed_in[k, 0] = chosen[:cap_rows]
        copies = []
        for d in range(1, groups):
            listed_out[k, d - 1] = chosen[d * cap_rows : (d + 1) * cap_rows]
            copies.append(
                pltpu.make_async_remote_copy(
                    src_ref=listed_out.at[k, d - 1],
                    dst_ref=listed_in.at[k, d],
                    send_sem=list_send.at[k, d - 1],
                    recv_sem=list_recv.at[k, d - 1],
                    device_id={"chan": group_peers[d - 1]},
                    device_id_type=MESH,
                )
            )
            copies[-1].start()
        list_copies.append(copies)

    pair_copies = [
        pltpu.make_async_remote_copy(
            src_ref=terms_out.at[k, 1 - core],
            dst_ref=pair_in.at[k],
            send_sem=pair_send.at[k],
            recv_sem=pair_recv.at[k],
            device_id={"win": chip * 2 + 1 - core},
            device_id_type=MESH,
        )
        for k in range(CHUNKS)
    ]
    chip_copies = [
        [
            pltpu.make_async_remote_copy(
                src_ref=chip_out.at[k, chip_peers[d - 1]],
                dst_ref=chip_in.at[k, d - 1],
                send_sem=chip_send.at[k, d - 1],
                recv_sem=chip_recv.at[k, d - 1],
                device_id={"win": chip_peers[d - 1] * 2 + core},
                device_id_type=MESH,
            )
            for d in range(1, chips)
        ]
        for k in range(CHUNKS)
    ]

    def cross(k):
        for copy in list_copies[k]:
            copy.wait_recv()
        table = dot(pick, listed_in[k].reshape(groups * cap_rows, quarter))
        piece = min(partners, share_rows)
        for b in range(blocks):
            for i in range(homes):
                real = imag = None
                for w in range(win_dev):
                    at = w * per_win + blocks * partners + b * homes + i
                    home_re = table[at : at + 1, :eighth]
                    home_im = table[at : at + 1, eighth:]
                    at = w * per_win + b * partners
                    part_re = table[at : at + partners, :eighth]
                    part_im = table[at : at + partners, eighth:]
                    add_re = home_re * part_re + home_im * part_im
                    add_im = home_im * part_re - home_re * part_im
                    real = add_re if real is None else real + add_re
                    imag = add_im if imag is None else imag + add_im
                term = jnp.concatenate([real, imag], axis=1)
                for j in range(0, partners, piece):
                    row = (b * homes + i) * partners + j
                    owner, inner = row // share_rows, row % share_rows
                    at = (owner // 2) * pad_rows + inner
                    terms[k, owner % 2, at : at + piece, :] = term[j : j + piece]
        terms_out[k, 1 - core] = terms[k, 1 - core].astype(jnp.bfloat16)
        pair_copies[k].start()

    def across(k):
        pair_copies[k].wait_recv()
        total = terms[k, core] + pair_in[k].astype(jnp.float32)
        total = total.reshape(chips, pad_rows, quarter)
        chip_sum[k] = total
        chip_out[k] = total.astype(jnp.bfloat16)
        for copy in chip_copies[k]:
            copy.start()

    for k in range(CHUNKS):
        cross(k)
        if k:
            across(k - 1)
    across(CHUNKS - 1)

    loads[4].wait()
    loads[5].wait()
    loads[9].wait()
    parts = []
    for k in range(CHUNKS):
        for copy in chip_copies[k]:
            copy.wait_recv()
        total = chip_sum[k, chip]
        for d in range(1, chips):
            total = total + chip_in[k, d - 1].astype(jnp.float32)
        table = inv_even[k] if k < 2 else inv_odd[k - 2]
        both = dot(jnp.concatenate(halves(total), axis=0), table)
        parts.append(both[:pad_rows] + both[pad_rows:])
    even = jnp.concatenate([parts[0] + parts[1], parts[0] - parts[1]], axis=1)
    odd = parts[2] + parts[3]
    norm = 1.0 / math.sqrt(samples * win_dev * win_count)
    row = win * share_rows + lax.broadcasted_iota(jnp.int32, (pad_rows, 1), 0)
    block = sum([(row >= b * homes * partners).astype(jnp.int32) for b in range(1, blocks)])
    gain = jnp.where(block < live_ref[...], norm, 0.0)
    out_ref[:, :half] = ((even - odd) * gain)[:share_rows]
    out_ref[:, half:] = ((even + odd) * gain)[:share_rows]

    for k in range(CHUNKS):
        for copy in list_copies[k] + [pair_copies[k]] + chip_copies[k]:
            copy.wait_send()


def body(traces, needed, home_slot, partner_slot, live_blocks):
    chan_dev, win_dev, samples = traces.shape
    groups, win_count = lax.axis_size("chan"), lax.axis_size("win")
    listing = needed.shape[1]
    cap = 2 * listing // groups
    cap_rows = -(-win_dev * cap // 16) * 16
    blocks, homes = home_slot.shape
    partners = partner_slot.shape[1]
    chips = win_count // 2
    share_rows = blocks * homes * partners // win_count
    pad_rows = max(share_rows, 16)
    quarter = samples // 4
    fwd_even, fwd_odd, band, inv_even, inv_odd = tables(samples)
    dims = (groups, win_count, chan_dev, win_dev, samples, listing, cap, cap_rows, blocks, homes, partners)
    vmem = pl.BlockSpec(memory_space=pltpu.VMEM)
    hbm = pl.BlockSpec(memory_space=pltpu.HBM)
    bf16, f32 = jnp.bfloat16, jnp.float32
    return pl.pallas_call(
        functools.partial(kernel, dims),
        out_shape=jax.ShapeDtypeStruct((share_rows, samples), f32),
        in_specs=[hbm] * 10,
        out_specs=vmem,
        scratch_shapes=[
            pltpu.VMEM(needed.shape, jnp.int32),
            pltpu.VMEM(home_slot.shape, jnp.int32),
            pltpu.VMEM(partner_slot.shape, jnp.int32),
            pltpu.VMEM((1, 1), jnp.int32),
            pltpu.VMEM(traces.shape, f32),
            pltpu.VMEM(fwd_even.shape, bf16),
            pltpu.VMEM(fwd_odd.shape, bf16),
            pltpu.VMEM(band.shape, bf16),
            pltpu.VMEM(inv_even.shape, bf16),
            pltpu.VMEM(inv_odd.shape, bf16),
            pltpu.VMEM((CHUNKS, groups - 1, cap_rows, quarter), bf16),
            pltpu.VMEM((CHUNKS, groups, cap_rows, quarter), bf16),
            pltpu.VMEM((CHUNKS, 2, chips * pad_rows, quarter), f32),
            pltpu.VMEM((CHUNKS, 2, chips * pad_rows, quarter), bf16),
            pltpu.VMEM((CHUNKS, chips * pad_rows, quarter), bf16),
            pltpu.VMEM((CHUNKS, chips, pad_rows, quarter), f32),
            pltpu.VMEM((CHUNKS, chips, pad_rows, quarter), bf16),
            pltpu.VMEM((CHUNKS, chips - 1, pad_rows, quarter), bf16),
            pltpu.SemaphoreType.DMA((10,)),
            pltpu.SemaphoreType.DMA((CHUNKS, groups - 1)),
            pltpu.SemaphoreType.DMA((CHUNKS, groups - 1)),
            pltpu.SemaphoreType.DMA((CHUNKS,)),
            pltpu.SemaphoreType.DMA((CHUNKS,)),
            pltpu.SemaphoreType.DMA((CHUNKS, chips - 1)),
            pltpu.SemaphoreType.DMA((CHUNKS, chips - 1)),
        ],
        compiler_params=pltpu.CompilerParams(
            collective_id=0, has_side_effects=True, vmem_limit_bytes=64 * 1024 * 1024
        ),
        cost_estimate=pl.CostEstimate(
            flops=2_000_000_000, bytes_accessed=4_000_000, transcendentals=100_000
        ),
        name="whiten_cross_stack",
    )(
        traces,
        needed,
        home_slot,
        partner_slot,
        live_blocks.reshape(1, 1),
        jnp.asarray(fwd_even),
        jnp.asarray(fwd_odd),
        jnp.asarray(band),
        jnp.asarray(inv_even),
        jnp.asarray(inv_odd),
    )


def solution(mesh):
    placed = (P("chan", "win", None), P(), P("chan", None), P("chan", None), P("chan"))
    return jax.shard_map(
        body, mesh=mesh, in_specs=placed, out_specs=P(("chan", "win"), None), check_vma=False
    )
```

```python
import functools
import math

import jax
import jax.numpy as jnp
import ml_dtypes
import numpy as np
from jax import lax
from jax.experimental import pallas as pl
from jax.experimental.pallas import tpu as pltpu
from jax.sharding import PartitionSpec as P

MESH = pl.DeviceIdType.MESH
BAND_REACH = 64


def split_table(table):
    high = table.astype(np.float32).astype(ml_dtypes.bfloat16)
    low = (table - high.astype(np.float64)).astype(np.float32).astype(ml_dtypes.bfloat16)
    return high, low


@functools.lru_cache(maxsize=None)
def tables(samples):
    quarter, half = samples // 4, samples // 2
    eighth = samples // 8
    bins_a = np.arange(0, half, 4)
    bins_b = np.arange(2, half, 4)
    bins_o = np.arange(1, half, 2)

    def forward(length, bins):
        phase = (np.arange(length)[:, None] * bins[None, :] % samples) * (2.0 * np.pi / samples)
        return np.cos(phase), -np.sin(phase)

    def inverse(length, bins):
        phase = (bins[:, None] * np.arange(length)[None, :] % samples) * (2.0 * np.pi / samples)
        weight = np.where(bins == 0, 1.0, 2.0)[:, None]
        return weight * np.cos(phase), -weight * np.sin(phase)

    odd_cos, odd_sin = forward(half, bins_o)
    fwd_a = np.concatenate(forward(quarter, bins_a), axis=1)
    fwd_b = np.concatenate(forward(quarter, bins_b), axis=1)
    fwd_o = np.concatenate(
        [odd_cos[:, :eighth], odd_sin[:, :eighth], odd_cos[:, eighth:], odd_sin[:, eighth:]], axis=1
    )
    fwd_even = np.stack([x for t in (fwd_a, fwd_b) for x in split_table(t)])
    fwd_odd = np.stack(split_table(fwd_o))
    order = np.concatenate([bins_a, bins_b, bins_o])
    inside = np.abs(order[:, None] - order[None, :]) <= BAND_REACH
    band = inside.astype(np.float32).astype(ml_dtypes.bfloat16)
    inv_cos, inv_sin = inverse(half, bins_o)
    inv_even = np.stack(
        [
            split_table(np.concatenate(inverse(quarter, bins), axis=0))[0]
            for bins in (bins_a, bins_b)
        ]
    )
    inv_odd = np.stack(
        [
            split_table(np.concatenate([inv_cos[rows], inv_sin[rows]], axis=0))[0]
            for rows in (slice(0, eighth), slice(eighth, None))
        ]
    )
    return fwd_even, fwd_odd, band, inv_even, inv_odd


def dot(left, right):
    return jnp.dot(left, right, preferred_element_type=jnp.float32)


def halves(value):
    high = value.astype(jnp.bfloat16)
    low = (value - high.astype(jnp.float32)).astype(jnp.bfloat16)
    return high, low


def as_column(row):
    n = row.shape[1]
    eye = lax.broadcasted_iota(jnp.int32, (n, n), 0) == lax.broadcasted_iota(jnp.int32, (n, n), 1)
    return jnp.sum(jnp.where(eye, jnp.broadcast_to(row, (n, n)), 0), axis=1, keepdims=True)


def kernel(
    dims,
    traces_hbm,
    needed_hbm,
    home_hbm,
    partner_hbm,
    fwd_even_hbm,
    fwd_odd_hbm,
    band_hbm,
    inv_even_hbm,
    inv_odd_hbm,
    out_ref,
    needed_ref,
    home_ref,
    partner_ref,
    traces,
    fwd_even,
    fwd_odd,
    band,
    inv_even,
    inv_odd,
    listed_out,
    listed_in,
    terms,
    terms_out,
    terms_in,
    load_sem,
    list_send,
    list_recv,
    term_send,
    term_recv,
):
    groups, win_count, chan_dev, win_dev, samples, listing, cap, cap_rows, blocks, homes, partners = dims
    chips = win_count // 2
    pairs = blocks * homes * partners
    share_rows = pairs // win_count
    pad_rows = terms.shape[2]
    quarter, half, eighth = samples // 4, samples // 2, samples // 8
    group = lax.axis_index("chan")
    win = lax.axis_index("win")
    chip, core = win // 2, win % 2

    loads = [
        pltpu.make_async_copy(src, dst, load_sem.at[i])
        for i, (src, dst) in enumerate(
            (
                (traces_hbm, traces),
                (fwd_even_hbm, fwd_even),
                (fwd_odd_hbm, fwd_odd),
                (band_hbm, band),
                (inv_even_hbm, inv_even),
                (inv_odd_hbm, inv_odd),
                (needed_hbm, needed_ref),
                (home_hbm, home_ref),
                (partner_hbm, partner_ref),
            )
        )
    ]
    for i in (6, 7, 8, 0, 1, 2, 3, 4, 5):
        loads[i].start()

    barrier = pltpu.get_barrier_semaphore()
    cores = (core, 1 - core)
    list_peers = [(d, s) for s in range(2) for d in range(groups) if d or s]
    term_peers = [(d, s) for d in reversed(range(chips)) for s in range(2) if d or s]

    def list_id(d, s):
        return {"chan": lax.rem(group + d, groups), "win": chip * 2 + cores[s]}

    def term_index(d, s):
        return lax.rem(chip + d, chips) * 2 + cores[s]

    greeted = [list_id(d, s) for d, s in list_peers]
    greeted += [{"win": term_index(d, s)} for d, s in term_peers if d]
    for peer in greeted:
        pl.semaphore_signal(barrier, inc=1, device_id=peer, device_id_type=MESH)

    lanes = win_dev * chan_dev
    lane = lax.broadcasted_iota(jnp.int32, (1, lanes), 1)
    lane_win = sum([(lane >= w * chan_dev).astype(jnp.int32) for w in range(1, win_dev)])
    lane_chan = lane - lane_win * chan_dev
    first_mine = group * chan_dev
    place = lax.broadcasted_iota(jnp.int32, (listing, lanes), 0)
    out_row = lax.broadcasted_iota(jnp.int32, (cap_rows, lanes), 0)
    for i in (6, 7, 8):
        loads[i].wait()
    choose = []
    for d in range(groups):
        owner = lax.rem(group + d, groups)
        column = as_column(needed_ref[pl.ds(owner, 1), :])
        hit = column == (lane_chan + first_mine)
        found = jnp.sum(jnp.where(hit, place + 1, 0), axis=0, keepdims=True)
        begin = jnp.sum((column < first_mine).astype(jnp.int32), axis=0, keepdims=True)
        target = jnp.where(found > 0, found - 1 - begin + lane_win * cap, -1)
        choose.append(jnp.where(out_row == target, 1.0, 0.0))
    choose = jnp.concatenate(choose, axis=0).astype(jnp.bfloat16)

    loads[0].wait()
    rows = jnp.concatenate([traces[:, w, :] for w in range(win_dev)], axis=0)
    count = rows.shape[0]
    folded = rows[:, :half] + rows[:, half:]
    odd_in = rows[:, :half] - rows[:, half:]
    even_in = (folded[:, :quarter] + folded[:, quarter:], folded[:, :quarter] - folded[:, quarter:])

    def transform(value, high_table, low_table):
        high, low = halves(value)
        both = dot(jnp.concatenate([high, low], axis=0), high_table)
        return both[:count] + both[count:] + dot(high, low_table)

    loads[1].wait()
    spectra = [
        transform(even_in[0], fwd_even[0], fwd_even[1]),
        transform(even_in[1], fwd_even[2], fwd_even[3]),
    ]
    loads[2].wait()
    odd_out = transform(odd_in, fwd_odd[0], fwd_odd[1])
    spectra += [odd_out[:, :quarter], odd_out[:, quarter:]]
    power = jnp.concatenate([s[:, :eighth] ** 2 + s[:, eighth:] ** 2 for s in spectra], axis=1)
    loads[3].wait()
    both = dot(jnp.concatenate(halves(power), axis=0), band[...])
    spot = lax.broadcasted_iota(jnp.int32, (1, half), 1)
    bins = jnp.where(
        spot < eighth,
        spot * 4,
        jnp.where(spot < quarter, (spot - eighth) * 4 + 2, (spot - quarter) * 2 + 1),
    )
    members = jnp.minimum(bins + BAND_REACH, half - 1) - jnp.maximum(bins - BAND_REACH, 0) + 1
    smooth = (both[:count] + both[count:]) * (1.0 / members.astype(jnp.float32))
    factor = 1.0 / jnp.sqrt(smooth + 1e-05)

    pl.semaphore_wait(barrier, len(greeted))

    list_copies = []
    for h in range(2):
        for k in (h, 2 + h):
            scale = factor[:, k * eighth : (k + 1) * eighth]
            whitened = jnp.concatenate(
                [spectra[k][:, :eighth] * scale, spectra[k][:, eighth:] * scale], axis=1
            ).astype(jnp.bfloat16)
            chosen = dot(choose, whitened).astype(jnp.bfloat16)
            for d in range(groups):
                listed_out[k, d] = chosen[d * cap_rows : (d + 1) * cap_rows]
        copies = []
        for n, (d, s) in enumerate(list_peers):
            copies.append(
                pltpu.make_async_remote_copy(
                    src_ref=listed_out.at[cores[s] * 2 + h, d],
                    dst_ref=listed_in.at[h, s, d],
                    send_sem=list_send.at[h, n],
                    recv_sem=list_recv.at[h, n],
                    device_id=list_id(d, s),
                    device_id_type=MESH,
                )
            )
            copies[-1].start()
        list_copies.append(copies)
        listed_in[h, 0, 0] = listed_out[core * 2 + h, 0]

    mine = needed_ref[pl.ds(group, 1), :]
    arrived = lax.broadcasted_iota(jnp.int32, (1, groups * cap_rows), 1)
    code = jnp.full((1, groups * cap_rows), -1, jnp.int32)
    for d in range(groups):
        source = lax.rem(group + groups - d, groups)
        begin = jnp.sum(
            (mine < source * chan_dev).astype(jnp.int32), axis=1, keepdims=True
        )
        for w in range(win_dev):
            low = d * cap_rows + w * cap
            within = (arrived >= low) & (arrived < low + cap)
            code = jnp.where(within, arrived - low + begin + w * listing, code)
    wanted = [as_column(partner_ref[b : b + 1, :]) for b in range(blocks)]
    wanted += [as_column(home_ref[b : b + 1, :]) for b in range(blocks)]
    wanted = jnp.concatenate(wanted, axis=0)
    per_win = blocks * (homes + partners)
    wanted = jnp.concatenate([wanted + w * listing for w in range(win_dev)], axis=0)
    pick = jnp.where(wanted == code, 1.0, 0.0).astype(jnp.bfloat16)

    term_copies = []
    piece = min(partners, share_rows)
    for h in range(2):
        for copy in list_copies[h]:
            copy.wait_recv()
        tables = [dot(pick, listed_in[h, s].reshape(groups * cap_rows, quarter)) for s in range(2)]
        for b in range(blocks):
            for i in range(homes):
                real = imag = None
                for table in tables:
                    for w in range(win_dev):
                        at = w * per_win + blocks * partners + b * homes + i
                        home_re = table[at : at + 1, :eighth]
                        home_im = table[at : at + 1, eighth:]
                        at = w * per_win + b * partners
                        part_re = table[at : at + partners, :eighth]
                        part_im = table[at : at + partners, eighth:]
                        add_re = home_re * part_re + home_im * part_im
                        add_im = home_im * part_re - home_re * part_im
                        real = add_re if real is None else real + add_re
                        imag = add_im if imag is None else imag + add_im
                term = jnp.concatenate([real, imag], axis=1)
                for j in range(0, partners, piece):
                    row = (b * homes + i) * partners + j
                    owner, inner = row // share_rows, row % share_rows
                    terms[h, owner, inner : inner + piece, :] = term[j : j + piece]
        terms_out[h] = terms[h].astype(jnp.bfloat16)
        copies = []
        for n, (d, s) in enumerate(term_peers):
            copies.append(
                pltpu.make_async_remote_copy(
                    src_ref=terms_out.at[h, term_index(d, s)],
                    dst_ref=terms_in.at[h, n],
                    send_sem=term_send.at[h, n],
                    recv_sem=term_recv.at[h, n],
                    device_id={"win": term_index(d, s)},
                    device_id_type=MESH,
                )
            )
            copies[-1].start()
        term_copies.append(copies)

    loads[4].wait()
    loads[5].wait()
    parts = [None] * 4
    for h in range(2):
        total = [terms[h, win], None]
        for n, (d, s) in enumerate(term_peers):
            term_copies[h][n].wait_recv()
            arrival = terms_in[h, n].astype(jnp.float32)
            total[s] = arrival if total[s] is None else total[s] + arrival
        for k, value in (
            (h, jnp.where(core == 0, total[0], total[1])),
            (2 + h, jnp.where(core == 0, total[1], total[0])),
        ):
            table = inv_even[h] if k < 2 else inv_odd[h]
            both = dot(jnp.concatenate(halves(value), axis=0), table)
            parts[k] = both[:pad_rows] + both[pad_rows:]
    even = jnp.concatenate([parts[0] + parts[1], parts[0] - parts[1]], axis=1)
    odd = parts[2] + parts[3]
    norm = 1.0 / math.sqrt(samples * win_dev * win_count)
    out_ref[:, :half] = ((even - odd) * norm)[:share_rows]
    out_ref[:, half:] = ((even + odd) * norm)[:share_rows]

    for copies in list_copies + term_copies:
        for copy in copies:
            copy.wait_send()


def body(traces, needed, home_slot, partner_slot, live_blocks):
    chan_dev, win_dev, samples = traces.shape
    groups, win_count = lax.axis_size("chan"), lax.axis_size("win")
    listing = needed.shape[1]
    cap = 2 * listing // groups
    cap_rows = -(-win_dev * cap // 16) * 16
    blocks, homes = home_slot.shape
    partners = partner_slot.shape[1]
    share_rows = blocks * homes * partners // win_count
    pad_rows = max(share_rows, 16)
    quarter = samples // 4
    fwd_even, fwd_odd, band, inv_even, inv_odd = tables(samples)
    dims = (groups, win_count, chan_dev, win_dev, samples, listing, cap, cap_rows, blocks, homes, partners)
    vmem = pl.BlockSpec(memory_space=pltpu.VMEM)
    hbm = pl.BlockSpec(memory_space=pltpu.HBM)
    bf16, f32 = jnp.bfloat16, jnp.float32
    stacked = pl.pallas_call(
        functools.partial(kernel, dims),
        out_shape=jax.ShapeDtypeStruct((share_rows, samples), f32),
        in_specs=[hbm] * 9,
        out_specs=vmem,
        scratch_shapes=[
            pltpu.VMEM(needed.shape, jnp.int32),
            pltpu.VMEM(home_slot.shape, jnp.int32),
            pltpu.VMEM(partner_slot.shape, jnp.int32),
            pltpu.VMEM(traces.shape, f32),
            pltpu.VMEM(fwd_even.shape, bf16),
            pltpu.VMEM(fwd_odd.shape, bf16),
            pltpu.VMEM(band.shape, bf16),
            pltpu.VMEM(inv_even.shape, bf16),
            pltpu.VMEM(inv_odd.shape, bf16),
            pltpu.VMEM((4, groups, cap_rows, quarter), bf16),
            pltpu.VMEM((2, 2, groups, cap_rows, quarter), bf16),
            pltpu.VMEM((2, win_count, pad_rows, quarter), f32),
            pltpu.VMEM((2, win_count, pad_rows, quarter), bf16),
            pltpu.VMEM((2, win_count - 1, pad_rows, quarter), bf16),
            pltpu.SemaphoreType.DMA((9,)),
            pltpu.SemaphoreType.DMA((2, 2 * groups - 1)),
            pltpu.SemaphoreType.DMA((2, 2 * groups - 1)),
            pltpu.SemaphoreType.DMA((2, win_count - 1)),
            pltpu.SemaphoreType.DMA((2, win_count - 1)),
        ],
        compiler_params=pltpu.CompilerParams(
            collective_id=0, has_side_effects=True, vmem_limit_bytes=64 * 1024 * 1024
        ),
        cost_estimate=pl.CostEstimate(
            flops=2_000_000_000, bytes_accessed=4_000_000, transcendentals=100_000
        ),
        name="whiten_cross_stack",
    )(
        traces,
        needed,
        home_slot,
        partner_slot,
        jnp.asarray(fwd_even),
        jnp.asarray(fwd_odd),
        jnp.asarray(band),
        jnp.asarray(inv_even),
        jnp.asarray(inv_odd),
    )
    row = lax.axis_index("win") * share_rows + lax.broadcasted_iota(jnp.int32, (share_rows, 1), 0)
    return stacked * (row // (homes * partners) < live_blocks[0]).astype(f32)


def solution(mesh):
    placed = (P("chan", "win", None), P(), P("chan", None), P("chan", None), P("chan"))
    return jax.shard_map(
        body, mesh=mesh, in_specs=placed, out_specs=P(("chan", "win"), None), check_vma=False
    )
```

```python
import functools
import math

import jax
import jax.numpy as jnp
import ml_dtypes
import numpy as np
from jax import lax
from jax.experimental import pallas as pl
from jax.experimental.pallas import tpu as pltpu
from jax.sharding import PartitionSpec as P

MESH = pl.DeviceIdType.MESH
BAND_REACH = 64
PIECES = 4


def split_table(table):
    high = table.astype(np.float32).astype(ml_dtypes.bfloat16)
    low = (table - high.astype(np.float64)).astype(np.float32).astype(ml_dtypes.bfloat16)
    return high, low


@functools.lru_cache(maxsize=None)
def tables(samples):
    quarter, half = samples // 4, samples // 2
    eighth = samples // 8
    bins_a = np.arange(0, half, 4)
    bins_b = np.arange(2, half, 4)
    bins_o = np.arange(1, half, 2)

    def forward(length, bins):
        phase = (np.arange(length)[:, None] * bins[None, :] % samples) * (2.0 * np.pi / samples)
        return np.cos(phase), -np.sin(phase)

    def inverse(length, bins):
        phase = (bins[:, None] * np.arange(length)[None, :] % samples) * (2.0 * np.pi / samples)
        weight = np.where(bins == 0, 1.0, 2.0)[:, None]
        return weight * np.cos(phase), -weight * np.sin(phase)

    odd_cos, odd_sin = forward(half, bins_o)
    fwd_a = np.concatenate(forward(quarter, bins_a), axis=1)
    fwd_b = np.concatenate(forward(quarter, bins_b), axis=1)
    fwd_o = np.concatenate(
        [odd_cos[:, :eighth], odd_sin[:, :eighth], odd_cos[:, eighth:], odd_sin[:, eighth:]], axis=1
    )
    fwd_even = np.stack([x for t in (fwd_a, fwd_b) for x in split_table(t)])
    fwd_odd = np.stack(split_table(fwd_o))
    order = np.concatenate([bins_a, bins_b, bins_o])
    inside = np.abs(order[:, None] - order[None, :]) <= BAND_REACH
    band = inside.astype(np.float32).astype(ml_dtypes.bfloat16)
    piece = eighth // 2

    def pieces(length, bins):
        cos, sin = inverse(length, bins)
        return [
            split_table(np.concatenate([cos[at : at + piece], sin[at : at + piece]], axis=0))[0]
            for at in range(0, len(bins), piece)
        ]

    inv_even = np.stack(pieces(quarter, bins_a) + pieces(quarter, bins_b))
    inv_odd = np.stack(pieces(half, bins_o))
    return fwd_even, fwd_odd, band, inv_even, inv_odd


def dot(left, right):
    return jnp.dot(left, right, preferred_element_type=jnp.float32)


def halves(value):
    high = value.astype(jnp.bfloat16)
    low = (value - high.astype(jnp.float32)).astype(jnp.bfloat16)
    return high, low


def as_column(row):
    n = row.shape[1]
    eye = lax.broadcasted_iota(jnp.int32, (n, n), 0) == lax.broadcasted_iota(jnp.int32, (n, n), 1)
    return jnp.sum(jnp.where(eye, jnp.broadcast_to(row, (n, n)), 0), axis=1, keepdims=True)


def kernel(
    dims,
    traces_hbm,
    needed_hbm,
    home_hbm,
    partner_hbm,
    live_ref,
    fwd_even_hbm,
    fwd_odd_hbm,
    band_hbm,
    inv_even_hbm,
    inv_odd_hbm,
    out_ref,
    needed_ref,
    home_ref,
    partner_ref,
    traces,
    fwd_even,
    fwd_odd,
    band,
    inv_even,
    inv_odd,
    listed_out,
    listed_in,
    terms,
    terms_out,
    terms_in,
    load_sem,
    list_send,
    list_recv,
    term_send,
    term_recv,
):
    groups, win_count, chan_dev, win_dev, samples, listing, cap, cap_rows, blocks, homes, partners = dims
    chips = win_count // 2
    pairs = blocks * homes * partners
    share_rows = pairs // win_count
    pad_rows = terms.shape[2]
    quarter, half, eighth = samples // 4, samples // 2, samples // 8
    group = lax.axis_index("chan")
    win = lax.axis_index("win")
    chip, core = win // 2, win % 2

    loads = [
        pltpu.make_async_copy(src, dst, load_sem.at[i])
        for i, (src, dst) in enumerate(
            (
                (traces_hbm, traces),
                (fwd_even_hbm, fwd_even),
                (fwd_odd_hbm, fwd_odd),
                (band_hbm, band),
                (inv_even_hbm, inv_even),
                (inv_odd_hbm, inv_odd),
                (needed_hbm, needed_ref),
                (home_hbm, home_ref),
                (partner_hbm, partner_ref),
            )
        )
    ]
    for i in (6, 7, 8, 0, 1, 2, 3, 4, 5):
        loads[i].start()

    barrier = pltpu.get_barrier_semaphore()
    cores = (core, 1 - core)
    list_peers = [(d, s) for s in range(2) for d in range(groups) if d or s]
    term_peers = [(d, s) for d in reversed(range(chips)) for s in range(2) if d or s]

    def list_id(d, s):
        return {"chan": lax.rem(group + d, groups), "win": chip * 2 + cores[s]}

    def term_index(d, s):
        return lax.rem(chip + d, chips) * 2 + cores[s]

    greeted = [list_id(d, s) for d, s in list_peers]
    greeted += [{"win": term_index(d, s)} for d, s in term_peers if d]
    for peer in greeted:
        pl.semaphore_signal(barrier, inc=1, device_id=peer, device_id_type=MESH)

    lanes = win_dev * chan_dev
    lane = lax.broadcasted_iota(jnp.int32, (1, lanes), 1)
    lane_win = sum([(lane >= w * chan_dev).astype(jnp.int32) for w in range(1, win_dev)])
    lane_chan = lane - lane_win * chan_dev
    first_mine = group * chan_dev
    place = lax.broadcasted_iota(jnp.int32, (listing, lanes), 0)
    out_row = lax.broadcasted_iota(jnp.int32, (cap_rows, lanes), 0)
    for i in (6, 7, 8):
        loads[i].wait()
    choose = []
    for d in range(groups):
        owner = lax.rem(group + d, groups)
        column = as_column(needed_ref[pl.ds(owner, 1), :])
        hit = column == (lane_chan + first_mine)
        found = jnp.sum(jnp.where(hit, place + 1, 0), axis=0, keepdims=True)
        begin = jnp.sum((column < first_mine).astype(jnp.int32), axis=0, keepdims=True)
        target = jnp.where(found > 0, found - 1 - begin + lane_win * cap, -1)
        choose.append(jnp.where(out_row == target, 1.0, 0.0))
    choose = jnp.concatenate(choose, axis=0).astype(jnp.bfloat16)

    loads[0].wait()
    rows = jnp.concatenate([traces[:, w, :] for w in range(win_dev)], axis=0)
    count = rows.shape[0]
    folded = rows[:, :half] + rows[:, half:]
    odd_in = rows[:, :half] - rows[:, half:]
    even_in = (folded[:, :quarter] + folded[:, quarter:], folded[:, :quarter] - folded[:, quarter:])

    def transform(value, high_table, low_table):
        high, low = halves(value)
        both = dot(jnp.concatenate([high, low], axis=0), high_table)
        return both[:count] + both[count:] + dot(high, low_table)

    loads[1].wait()
    spectra = [
        transform(even_in[0], fwd_even[0], fwd_even[1]),
        transform(even_in[1], fwd_even[2], fwd_even[3]),
    ]
    loads[2].wait()
    odd_out = transform(odd_in, fwd_odd[0], fwd_odd[1])
    spectra += [odd_out[:, :quarter], odd_out[:, quarter:]]
    power = jnp.concatenate([s[:, :eighth] ** 2 + s[:, eighth:] ** 2 for s in spectra], axis=1)
    loads[3].wait()
    both = dot(jnp.concatenate(halves(power), axis=0), band[...])
    spot = lax.broadcasted_iota(jnp.int32, (1, half), 1)
    bins = jnp.where(
        spot < eighth,
        spot * 4,
        jnp.where(spot < quarter, (spot - eighth) * 4 + 2, (spot - quarter) * 2 + 1),
    )
    members = jnp.minimum(bins + BAND_REACH, half - 1) - jnp.maximum(bins - BAND_REACH, 0) + 1
    smooth = (both[:count] + both[count:]) * (1.0 / members.astype(jnp.float32))
    factor = lax.rsqrt(smooth + 1e-05)

    pl.semaphore_wait(barrier, len(greeted))

    first_half = lax.broadcasted_iota(jnp.int32, (1, eighth), 1) < eighth // 2

    def swap(value):
        return pltpu.roll(value, eighth // 2, 1)

    list_copies = []
    for h in range(PIECES):
        if h % 2 == 0:
            for half_at in range(2):
                k = half_at * 2 + h // 2
                scale = factor[:, k * eighth : (k + 1) * eighth]
                whitened = jnp.concatenate(
                    [spectra[k][:, :eighth] * scale, spectra[k][:, eighth:] * scale], axis=1
                ).astype(jnp.bfloat16)
                chosen = dot(choose, whitened)
                real, imag = chosen[:, :eighth], chosen[:, eighth:]
                for j, value in enumerate(
                    (jnp.where(first_half, real, swap(imag)), jnp.where(first_half, swap(real), imag))
                ):
                    value = value.astype(jnp.bfloat16)
                    for d in range(groups):
                        listed_out[half_at, h + j, d] = value[d * cap_rows : (d + 1) * cap_rows]
        copies = []
        for n, (d, s) in enumerate(list_peers):
            copies.append(
                pltpu.make_async_remote_copy(
                    src_ref=listed_out.at[cores[s], h, d],
                    dst_ref=listed_in.at[h, s, d],
                    send_sem=list_send.at[h, n],
                    recv_sem=list_recv.at[h, n],
                    device_id=list_id(d, s),
                    device_id_type=MESH,
                )
            )
            copies[-1].start()
        list_copies.append(copies)
        listed_in[h, 0, 0] = listed_out[core, h, 0]

    mine = needed_ref[pl.ds(group, 1), :]
    arrived = lax.broadcasted_iota(jnp.int32, (1, groups * cap_rows), 1)
    code = jnp.full((1, groups * cap_rows), -1, jnp.int32)
    for d in range(groups):
        source = lax.rem(group + groups - d, groups)
        begin = jnp.sum(
            (mine < source * chan_dev).astype(jnp.int32), axis=1, keepdims=True
        )
        for w in range(win_dev):
            low = d * cap_rows + w * cap
            within = (arrived >= low) & (arrived < low + cap)
            code = jnp.where(within, arrived - low + begin + w * listing, code)
    wanted = [as_column(partner_ref[b : b + 1, :]) for b in range(blocks)]
    wanted += [as_column(home_ref[b : b + 1, :]) for b in range(blocks)]
    wanted = jnp.concatenate(wanted, axis=0)
    per_win = blocks * (homes + partners)
    wanted = jnp.concatenate([wanted + w * listing for w in range(win_dev)], axis=0)
    pick = jnp.where(wanted == code, 1.0, 0.0).astype(jnp.bfloat16)

    term_copies = []
    piece = min(partners, share_rows)
    for h in range(PIECES):
        for copy in list_copies[h]:
            copy.wait_recv()
        tables = [dot(pick, listed_in[h, s].reshape(groups * cap_rows, eighth)) for s in range(2)]
        swapped = [swap(table) for table in tables]
        for b in range(blocks):
            for i in range(homes):
                straight = crossed = None
                for table, other in zip(tables, swapped):
                    for w in range(win_dev):
                        at = w * per_win + blocks * partners + b * homes + i
                        home = table[at : at + 1]
                        at = w * per_win + b * partners
                        add = home * table[at : at + partners]
                        straight = add if straight is None else straight + add
                        add = home * other[at : at + partners]
                        crossed = add if crossed is None else crossed + add
                term = jnp.where(first_half, straight + swap(straight), crossed - swap(crossed))
                for j in range(0, partners, piece):
                    row = (b * homes + i) * partners + j
                    owner, inner = row // share_rows, row % share_rows
                    terms[h, owner, inner : inner + piece, :] = term[j : j + piece]
        terms_out[h] = terms[h].astype(jnp.bfloat16)
        copies = []
        for n, (d, s) in enumerate(term_peers):
            copies.append(
                pltpu.make_async_remote_copy(
                    src_ref=terms_out.at[h, term_index(d, s)],
                    dst_ref=terms_in.at[h, n],
                    send_sem=term_send.at[h, n],
                    recv_sem=term_recv.at[h, n],
                    device_id={"win": term_index(d, s)},
                    device_id_type=MESH,
                )
            )
            copies[-1].start()
        term_copies.append(copies)

    loads[4].wait()
    loads[5].wait()
    parts = [[], [], []]
    for h in range(PIECES):
        total = [terms[h, win], None]
        for n, (d, s) in enumerate(term_peers):
            term_copies[h][n].wait_recv()
            arrival = terms_in[h, n].astype(jnp.float32)
            total[s] = arrival if total[s] is None else total[s] + arrival
        for value, table, part in (
            (jnp.where(core == 0, total[0], total[1]), inv_even[h], h // 2),
            (jnp.where(core == 0, total[1], total[0]), inv_odd[h], 2),
        ):
            both = dot(jnp.concatenate(halves(value), axis=0), table)
            parts[part].append(both[:pad_rows] + both[pad_rows:])
    parts = [sum(part) for part in parts]
    even = jnp.concatenate([parts[0] + parts[1], parts[0] - parts[1]], axis=1)
    odd = parts[2]
    norm = 1.0 / math.sqrt(samples * win_dev * win_count)
    row = win * share_rows + lax.broadcasted_iota(jnp.int32, (pad_rows, 1), 0)
    norm = jnp.where(row < live_ref[0] * (homes * partners), norm, 0.0)
    out_ref[:, :half] = ((even - odd) * norm)[:share_rows]
    out_ref[:, half:] = ((even + odd) * norm)[:share_rows]

    for copies in list_copies + term_copies:
        for copy in copies:
            copy.wait_send()


def body(traces, needed, home_slot, partner_slot, live_blocks):
    chan_dev, win_dev, samples = traces.shape
    groups, win_count = lax.axis_size("chan"), lax.axis_size("win")
    listing = needed.shape[1]
    cap = 2 * listing // groups
    cap_rows = -(-win_dev * cap // 16) * 16
    blocks, homes = home_slot.shape
    partners = partner_slot.shape[1]
    share_rows = blocks * homes * partners // win_count
    pad_rows = max(share_rows, 16)
    eighth = samples // 8
    fwd_even, fwd_odd, band, inv_even, inv_odd = tables(samples)
    dims = (groups, win_count, chan_dev, win_dev, samples, listing, cap, cap_rows, blocks, homes, partners)
    vmem = pl.BlockSpec(memory_space=pltpu.VMEM)
    smem = pl.BlockSpec(memory_space=pltpu.SMEM)
    hbm = pl.BlockSpec(memory_space=pltpu.HBM)
    bf16, f32 = jnp.bfloat16, jnp.float32
    return pl.pallas_call(
        functools.partial(kernel, dims),
        out_shape=jax.ShapeDtypeStruct((share_rows, samples), f32),
        in_specs=[hbm] * 4 + [smem] + [hbm] * 5,
        out_specs=vmem,
        scratch_shapes=[
            pltpu.VMEM(needed.shape, jnp.int32),
            pltpu.VMEM(home_slot.shape, jnp.int32),
            pltpu.VMEM(partner_slot.shape, jnp.int32),
            pltpu.VMEM(traces.shape, f32),
            pltpu.VMEM(fwd_even.shape, bf16),
            pltpu.VMEM(fwd_odd.shape, bf16),
            pltpu.VMEM(band.shape, bf16),
            pltpu.VMEM(inv_even.shape, bf16),
            pltpu.VMEM(inv_odd.shape, bf16),
            pltpu.VMEM((2, PIECES, groups, cap_rows, eighth), bf16),
            pltpu.VMEM((PIECES, 2, groups, cap_rows, eighth), bf16),
            pltpu.VMEM((PIECES, win_count, pad_rows, eighth), f32),
            pltpu.VMEM((PIECES, win_count, pad_rows, eighth), bf16),
            pltpu.VMEM((PIECES, win_count - 1, pad_rows, eighth), bf16),
            pltpu.SemaphoreType.DMA((9,)),
            pltpu.SemaphoreType.DMA((PIECES, 2 * groups - 1)),
            pltpu.SemaphoreType.DMA((PIECES, 2 * groups - 1)),
            pltpu.SemaphoreType.DMA((PIECES, win_count - 1)),
            pltpu.SemaphoreType.DMA((PIECES, win_count - 1)),
        ],
        compiler_params=pltpu.CompilerParams(
            collective_id=0, has_side_effects=True, vmem_limit_bytes=64 * 1024 * 1024
        ),
        cost_estimate=pl.CostEstimate(
            flops=2_000_000_000, bytes_accessed=4_000_000, transcendentals=100_000
        ),
        name="whiten_cross_stack",
    )(
        traces,
        needed,
        home_slot,
        partner_slot,
        live_blocks,
        jnp.asarray(fwd_even),
        jnp.asarray(fwd_odd),
        jnp.asarray(band),
        jnp.asarray(inv_even),
        jnp.asarray(inv_odd),
    )
def solution(mesh):
    placed = (P("chan", "win", None), P(), P("chan", None), P("chan", None), P("chan"))
    return jax.shard_map(
        body, mesh=mesh, in_specs=placed, out_specs=P(("chan", "win"), None), check_vma=False
    )
```

```python
import functools
import math

import jax
import jax.numpy as jnp
import ml_dtypes
import numpy as np
from jax import lax
from jax.experimental import pallas as pl
from jax.experimental.pallas import tpu as pltpu
from jax.sharding import PartitionSpec as P

MESH = pl.DeviceIdType.MESH
BAND_REACH = 64


def split_table(table):
    high = table.astype(np.float32).astype(ml_dtypes.bfloat16)
    low = (table - high.astype(np.float64)).astype(np.float32).astype(ml_dtypes.bfloat16)
    return high, low


@functools.lru_cache(maxsize=None)
def tables(samples):
    quarter, half = samples // 4, samples // 2
    eighth = samples // 8
    bins_a = np.arange(0, half, 4)
    bins_b = np.arange(2, half, 4)
    bins_o = np.arange(1, half, 2)

    def forward(length, bins):
        phase = (np.arange(length)[:, None] * bins[None, :] % samples) * (2.0 * np.pi / samples)
        return np.cos(phase), -np.sin(phase)

    def inverse(length, bins):
        phase = (bins[:, None] * np.arange(length)[None, :] % samples) * (2.0 * np.pi / samples)
        weight = np.where(bins == 0, 1.0, 2.0)[:, None]
        return weight * np.cos(phase), -weight * np.sin(phase)

    odd_cos, odd_sin = forward(half, bins_o)
    fwd_a = np.concatenate(forward(quarter, bins_a), axis=1)
    fwd_b = np.concatenate(forward(quarter, bins_b), axis=1)
    fwd_o = np.concatenate(
        [odd_cos[:, :eighth], odd_sin[:, :eighth], odd_cos[:, eighth:], odd_sin[:, eighth:]], axis=1
    )
    fwd_even = np.stack([x for t in (fwd_a, fwd_b) for x in split_table(t)])
    fwd_odd = np.stack(split_table(fwd_o))
    order = np.concatenate([bins_a, bins_b, bins_o])
    inside = np.abs(order[:, None] - order[None, :]) <= BAND_REACH
    band = inside.astype(np.float32).astype(ml_dtypes.bfloat16)
    inv_cos, inv_sin = inverse(half, bins_o)
    inv_even = np.stack(
        [
            split_table(np.concatenate(inverse(quarter, bins), axis=0))[0]
            for bins in (bins_a, bins_b)
        ]
    )
    inv_odd = np.stack(
        [
            split_table(np.concatenate([inv_cos[rows], inv_sin[rows]], axis=0))[0]
            for rows in (slice(0, eighth), slice(eighth, None))
        ]
    )
    return fwd_even, fwd_odd, band, inv_even, inv_odd


def dot(left, right):
    return jnp.dot(left, right, preferred_element_type=jnp.float32)


def halves(value):
    high = value.astype(jnp.bfloat16)
    low = (value - high.astype(jnp.float32)).astype(jnp.bfloat16)
    return high, low


def as_column(row):
    n = row.shape[1]
    eye = lax.broadcasted_iota(jnp.int32, (n, n), 0) == lax.broadcasted_iota(jnp.int32, (n, n), 1)
    return jnp.sum(jnp.where(eye, jnp.broadcast_to(row, (n, n)), 0), axis=1, keepdims=True)


def kernel(
    dims,
    traces_hbm,
    needed_hbm,
    home_hbm,
    partner_hbm,
    live_ref,
    fwd_even_hbm,
    fwd_odd_hbm,
    band_hbm,
    inv_even_hbm,
    inv_odd_hbm,
    out_ref,
    needed_ref,
    home_ref,
    partner_ref,
    traces,
    fwd_even,
    fwd_odd,
    band,
    inv_even,
    inv_odd,
    listed_out,
    listed_in,
    terms,
    terms_out,
    terms_in,
    load_sem,
    list_send,
    list_recv,
    term_send,
    term_recv,
):
    groups, win_count, chan_dev, win_dev, samples, listing, cap, cap_rows, blocks, homes, partners = dims
    chips = win_count // 2
    pairs = blocks * homes * partners
    share_rows = pairs // win_count
    pad_rows = terms.shape[2]
    quarter, half, eighth = samples // 4, samples // 2, samples // 8
    group = lax.axis_index("chan")
    win = lax.axis_index("win")
    chip, core = win // 2, win % 2

    loads = [
        pltpu.make_async_copy(src, dst, load_sem.at[i])
        for i, (src, dst) in enumerate(
            (
                (traces_hbm, traces),
                (fwd_even_hbm, fwd_even),
                (fwd_odd_hbm, fwd_odd),
                (band_hbm, band),
                (inv_even_hbm, inv_even),
                (inv_odd_hbm, inv_odd),
                (needed_hbm, needed_ref),
                (home_hbm, home_ref),
                (partner_hbm, partner_ref),
            )
        )
    ]
    for i in (6, 7, 8, 0, 1, 2, 3, 4, 5):
        loads[i].start()

    barrier = pltpu.get_barrier_semaphore()
    cores = (core, 1 - core)
    list_peers = [(d, s) for s in range(2) for d in range(groups) if d or s]
    term_peers = [(d, s) for d in reversed(range(chips)) for s in range(2) if d or s]

    def list_id(d, s):
        return {"chan": lax.rem(group + d, groups), "win": chip * 2 + cores[s]}

    def term_index(d, s):
        return lax.rem(chip + d, chips) * 2 + cores[s]

    greeted = [list_id(d, s) for d, s in list_peers]
    greeted += [{"win": term_index(d, s)} for d, s in term_peers if d]
    for peer in greeted:
        pl.semaphore_signal(barrier, inc=1, device_id=peer, device_id_type=MESH)

    lanes = win_dev * chan_dev
    lane = lax.broadcasted_iota(jnp.int32, (1, lanes), 1)
    lane_win = sum([(lane >= w * chan_dev).astype(jnp.int32) for w in range(1, win_dev)])
    lane_chan = lane - lane_win * chan_dev
    first_mine = group * chan_dev
    place = lax.broadcasted_iota(jnp.int32, (listing, lanes), 0)
    out_row = lax.broadcasted_iota(jnp.int32, (cap_rows, lanes), 0)
    for i in (6, 7, 8):
        loads[i].wait()
    choose = []
    for d in range(groups):
        owner = lax.rem(group + d, groups)
        column = as_column(needed_ref[pl.ds(owner, 1), :])
        hit = column == (lane_chan + first_mine)
        found = jnp.sum(jnp.where(hit, place + 1, 0), axis=0, keepdims=True)
        begin = jnp.sum((column < first_mine).astype(jnp.int32), axis=0, keepdims=True)
        target = jnp.where(found > 0, found - 1 - begin + lane_win * cap, -1)
        choose.append(jnp.where(out_row == target, 1.0, 0.0))
    choose = jnp.concatenate(choose, axis=0).astype(jnp.bfloat16)

    loads[0].wait()
    tiles = samples // 128
    rows = jnp.concatenate(
        [
            jnp.concatenate(
                [
                    traces[pl.ds(t * win_dev + w, chan_dev, stride=tiles * win_dev), :]
                    for t in range(tiles)
                ],
                axis=1,
            )
            for w in range(win_dev)
        ],
        axis=0,
    )
    count = rows.shape[0]
    folded = rows[:, :half] + rows[:, half:]
    odd_in = rows[:, :half] - rows[:, half:]
    even_in = (folded[:, :quarter] + folded[:, quarter:], folded[:, :quarter] - folded[:, quarter:])

    def transform(value, high_table, low_table):
        high, low = halves(value)
        both = dot(jnp.concatenate([high, low], axis=0), high_table)
        return both[:count] + both[count:] + dot(high, low_table)

    loads[1].wait()
    spectra = [
        transform(even_in[0], fwd_even[0], fwd_even[1]),
        transform(even_in[1], fwd_even[2], fwd_even[3]),
    ]
    loads[2].wait()
    odd_out = transform(odd_in, fwd_odd[0], fwd_odd[1])
    spectra += [odd_out[:, :quarter], odd_out[:, quarter:]]
    power = jnp.concatenate([s[:, :eighth] ** 2 + s[:, eighth:] ** 2 for s in spectra], axis=1)
    loads[3].wait()
    both = dot(jnp.concatenate(halves(power), axis=0), band[...])
    spot = lax.broadcasted_iota(jnp.int32, (1, half), 1)
    bins = jnp.where(
        spot < eighth,
        spot * 4,
        jnp.where(spot < quarter, (spot - eighth) * 4 + 2, (spot - quarter) * 2 + 1),
    )
    members = jnp.minimum(bins + BAND_REACH, half - 1) - jnp.maximum(bins - BAND_REACH, 0) + 1
    smooth = (both[:count] + both[count:]) * (1.0 / members.astype(jnp.float32))
    factor = lax.rsqrt(smooth + 1e-05)

    pl.semaphore_wait(barrier, len(greeted))

    list_copies = []
    for h in range(2):
        for k in (h, 2 + h):
            scale = factor[:, k * eighth : (k + 1) * eighth]
            whitened = jnp.concatenate(
                [spectra[k][:, :eighth] * scale, spectra[k][:, eighth:] * scale], axis=1
            ).astype(jnp.bfloat16)
            chosen = dot(choose, whitened).astype(jnp.bfloat16)
            for d in range(groups):
                listed_out[k, d] = chosen[d * cap_rows : (d + 1) * cap_rows]
        copies = []
        for n, (d, s) in enumerate(list_peers):
            copies.append(
                pltpu.make_async_remote_copy(
                    src_ref=listed_out.at[cores[s] * 2 + h, d],
                    dst_ref=listed_in.at[h, s, d],
                    send_sem=list_send.at[h, n],
                    recv_sem=list_recv.at[h, n],
                    device_id=list_id(d, s),
                    device_id_type=MESH,
                )
            )
            copies[-1].start()
        list_copies.append(copies)
        listed_in[h, 0, 0] = listed_out[core * 2 + h, 0]

    mine = needed_ref[pl.ds(group, 1), :]
    arrived = lax.broadcasted_iota(jnp.int32, (1, groups * cap_rows), 1)
    code = jnp.full((1, groups * cap_rows), -1, jnp.int32)
    for d in range(groups):
        source = lax.rem(group + groups - d, groups)
        begin = jnp.sum(
            (mine < source * chan_dev).astype(jnp.int32), axis=1, keepdims=True
        )
        for w in range(win_dev):
            low = d * cap_rows + w * cap
            within = (arrived >= low) & (arrived < low + cap)
            code = jnp.where(within, arrived - low + begin + w * listing, code)
    wanted = [as_column(partner_ref[b : b + 1, :]) for b in range(blocks)]
    wanted += [as_column(home_ref[b : b + 1, :]) for b in range(blocks)]
    wanted = jnp.concatenate(wanted, axis=0)
    per_win = blocks * (homes + partners)
    wanted = jnp.concatenate([wanted + w * listing for w in range(win_dev)], axis=0)
    pick = jnp.where(wanted == code, 1.0, 0.0).astype(jnp.bfloat16)

    term_copies = []
    piece = min(partners, share_rows)
    for h in range(2):
        for copy in list_copies[h]:
            copy.wait_recv()
        tables = [dot(pick, listed_in[h, s].reshape(groups * cap_rows, quarter)) for s in range(2)]
        for b in range(blocks):
            for i in range(homes):
                real = imag = None
                for table in tables:
                    for w in range(win_dev):
                        at = w * per_win + blocks * partners + b * homes + i
                        home_re = table[at : at + 1, :eighth]
                        home_im = table[at : at + 1, eighth:]
                        at = w * per_win + b * partners
                        part_re = table[at : at + partners, :eighth]
                        part_im = table[at : at + partners, eighth:]
                        add_re = home_re * part_re + home_im * part_im
                        add_im = home_im * part_re - home_re * part_im
                        real = add_re if real is None else real + add_re
                        imag = add_im if imag is None else imag + add_im
                term = jnp.concatenate([real, imag], axis=1)
                for j in range(0, partners, piece):
                    row = (b * homes + i) * partners + j
                    owner, inner = row // share_rows, row % share_rows
                    terms[h, owner, inner : inner + piece, :] = term[j : j + piece]
                    terms_out[h, owner, inner : inner + piece, :] = term[j : j + piece].astype(
                        jnp.bfloat16
                    )
        copies = []
        for n, (d, s) in enumerate(term_peers):
            copies.append(
                pltpu.make_async_remote_copy(
                    src_ref=terms_out.at[h, term_index(d, s)],
                    dst_ref=terms_in.at[h, n],
                    send_sem=term_send.at[h, n],
                    recv_sem=term_recv.at[h, n],
                    device_id={"win": term_index(d, s)},
                    device_id_type=MESH,
                )
            )
            copies[-1].start()
        term_copies.append(copies)

    loads[4].wait()
    loads[5].wait()
    for copies in list_copies:
        for copy in copies:
            copy.wait_send()
    parts = [None] * 4
    for h in range(2):
        total = [terms[h, win], None]
        for n, (d, s) in enumerate(term_peers):
            term_copies[h][n].wait_recv()
            arrival = terms_in[h, n].astype(jnp.float32)
            total[s] = arrival if total[s] is None else total[s] + arrival
        for k, value in (
            (h, jnp.where(core == 0, total[0], total[1])),
            (2 + h, jnp.where(core == 0, total[1], total[0])),
        ):
            table = inv_even[h] if k < 2 else inv_odd[h]
            both = dot(jnp.concatenate(halves(value), axis=0), table)
            parts[k] = both[:pad_rows] + both[pad_rows:]
    for copies in term_copies:
        for copy in copies:
            copy.wait_send()
    even = jnp.concatenate([parts[0] + parts[1], parts[0] - parts[1]], axis=1)
    odd = parts[2] + parts[3]
    norm = 1.0 / math.sqrt(samples * win_dev * win_count)
    row = win * share_rows + lax.broadcasted_iota(jnp.int32, (pad_rows, 1), 0)
    norm = jnp.where(row < live_ref[0] * (homes * partners), norm, 0.0)
    out_ref[:, :half] = ((even - odd) * norm)[:share_rows]
    out_ref[:, half:] = ((even + odd) * norm)[:share_rows]


def body(traces, needed, home_slot, partner_slot, live_blocks):
    chan_dev, win_dev, samples = traces.shape
    groups, win_count = lax.axis_size("chan"), lax.axis_size("win")
    listing = needed.shape[1]
    cap = 2 * listing // groups
    cap_rows = -(-win_dev * cap // 16) * 16
    blocks, homes = home_slot.shape
    partners = partner_slot.shape[1]
    share_rows = blocks * homes * partners // win_count
    pad_rows = max(share_rows, 16)
    quarter = samples // 4
    fwd_even, fwd_odd, band, inv_even, inv_odd = tables(samples)
    dims = (groups, win_count, chan_dev, win_dev, samples, listing, cap, cap_rows, blocks, homes, partners)
    tiled = traces.reshape(chan_dev, win_dev, samples // 128, 128).transpose(0, 2, 1, 3)
    tiled = tiled.reshape(-1, 128)
    vmem = pl.BlockSpec(memory_space=pltpu.VMEM)
    smem = pl.BlockSpec(memory_space=pltpu.SMEM)
    hbm = pl.BlockSpec(memory_space=pltpu.HBM)
    bf16, f32 = jnp.bfloat16, jnp.float32
    return pl.pallas_call(
        functools.partial(kernel, dims),
        out_shape=jax.ShapeDtypeStruct((share_rows, samples), f32),
        in_specs=[hbm] * 4 + [smem] + [hbm] * 5,
        out_specs=vmem,
        scratch_shapes=[
            pltpu.VMEM(needed.shape, jnp.int32),
            pltpu.VMEM(home_slot.shape, jnp.int32),
            pltpu.VMEM(partner_slot.shape, jnp.int32),
            pltpu.VMEM(tiled.shape, f32),
            pltpu.VMEM(fwd_even.shape, bf16),
            pltpu.VMEM(fwd_odd.shape, bf16),
            pltpu.VMEM(band.shape, bf16),
            pltpu.VMEM(inv_even.shape, bf16),
            pltpu.VMEM(inv_odd.shape, bf16),
            pltpu.VMEM((4, groups, cap_rows, quarter), bf16),
            pltpu.VMEM((2, 2, groups, cap_rows, quarter), bf16),
            pltpu.VMEM((2, win_count, pad_rows, quarter), f32),
            pltpu.VMEM((2, win_count, pad_rows, quarter), bf16),
            pltpu.VMEM((2, win_count - 1, pad_rows, quarter), bf16),
            pltpu.SemaphoreType.DMA((9,)),
            pltpu.SemaphoreType.DMA((2, 2 * groups - 1)),
            pltpu.SemaphoreType.DMA((2, 2 * groups - 1)),
            pltpu.SemaphoreType.DMA((2, win_count - 1)),
            pltpu.SemaphoreType.DMA((2, win_count - 1)),
        ],
        compiler_params=pltpu.CompilerParams(
            collective_id=0, has_side_effects=True, vmem_limit_bytes=64 * 1024 * 1024
        ),
        cost_estimate=pl.CostEstimate(
            flops=2_000_000_000, bytes_accessed=4_000_000, transcendentals=100_000
        ),
        name="whiten_cross_stack",
    )(
        tiled,
        needed,
        home_slot,
        partner_slot,
        live_blocks,
        jnp.asarray(fwd_even),
        jnp.asarray(fwd_odd),
        jnp.asarray(band),
        jnp.asarray(inv_even),
        jnp.asarray(inv_odd),
    )


def solution(mesh):
    placed = (P("chan", "win", None), P(), P("chan", None), P("chan", None), P("chan"))
    return jax.shard_map(
        body, mesh=mesh, in_specs=placed, out_specs=P(("chan", "win"), None), check_vma=False
    )
```

```python
import functools
import math

import jax
import jax.numpy as jnp
import ml_dtypes
import numpy as np
from jax import lax
from jax.experimental import pallas as pl
from jax.experimental.pallas import tpu as pltpu
from jax.sharding import PartitionSpec as P

MESH = pl.DeviceIdType.MESH
BAND_REACH = 64


def split_table(table):
    high = table.astype(np.float32).astype(ml_dtypes.bfloat16)
    low = (table - high.astype(np.float64)).astype(np.float32).astype(ml_dtypes.bfloat16)
    return high, low


@functools.lru_cache(maxsize=None)
def tables(samples):
    quarter, half = samples // 4, samples // 2
    eighth = samples // 8
    bins_a = np.arange(0, half, 4)
    bins_b = np.arange(2, half, 4)
    bins_o = np.arange(1, half, 2)

    def forward(length, bins):
        phase = (np.arange(length)[:, None] * bins[None, :] % samples) * (2.0 * np.pi / samples)
        return np.cos(phase), -np.sin(phase)

    def inverse(length, bins):
        phase = (bins[:, None] * np.arange(length)[None, :] % samples) * (2.0 * np.pi / samples)
        weight = np.where(bins == 0, 1.0, 2.0)[:, None]
        return weight * np.cos(phase), -weight * np.sin(phase)

    odd_cos, odd_sin = forward(half, bins_o)
    fwd_a = np.concatenate(forward(quarter, bins_a), axis=1)
    fwd_b = np.concatenate(forward(quarter, bins_b), axis=1)
    fwd_o = np.concatenate(
        [odd_cos[:, :eighth], odd_sin[:, :eighth], odd_cos[:, eighth:], odd_sin[:, eighth:]], axis=1
    )
    fwd_even = np.stack([x for t in (fwd_a, fwd_b) for x in split_table(t)])
    fwd_odd = np.stack(split_table(fwd_o))
    order = np.concatenate([bins_a, bins_b, bins_o])
    inside = np.abs(order[:, None] - order[None, :]) <= BAND_REACH
    band = inside.astype(np.float32).astype(ml_dtypes.bfloat16)
    inv_cos, inv_sin = inverse(half, bins_o)
    inv_even = np.stack(
        [
            split_table(np.concatenate(inverse(quarter, bins), axis=0))[0]
            for bins in (bins_a, bins_b)
        ]
    )
    inv_odd = np.stack(
        [
            split_table(np.concatenate([inv_cos[rows], inv_sin[rows]], axis=0))[0]
            for rows in (slice(0, eighth), slice(eighth, None))
        ]
    )
    return fwd_even, fwd_odd, band, inv_even, inv_odd


def dot(left, right):
    return jnp.dot(left, right, preferred_element_type=jnp.float32)


def halves(value):
    high = value.astype(jnp.bfloat16)
    low = (value - high.astype(jnp.float32)).astype(jnp.bfloat16)
    return high, low


def as_column(row):
    n = row.shape[1]
    eye = lax.broadcasted_iota(jnp.int32, (n, n), 0) == lax.broadcasted_iota(jnp.int32, (n, n), 1)
    return jnp.sum(jnp.where(eye, jnp.broadcast_to(row, (n, n)), 0), axis=1, keepdims=True)


def kernel(
    dims,
    traces_hbm,
    needed_hbm,
    home_hbm,
    partner_hbm,
    live_ref,
    fwd_even_hbm,
    fwd_odd_hbm,
    band_hbm,
    inv_even_hbm,
    inv_odd_hbm,
    out_ref,
    needed_ref,
    home_ref,
    partner_ref,
    traces,
    fwd_even,
    fwd_odd,
    band,
    inv_even,
    inv_odd,
    listed_out,
    listed_in,
    last_in,
    load_sem,
    list_send,
    list_recv,
    fold_send,
    fold_recv,
    last_send,
    last_recv,
    *fold_refs,
):
    groups, win_count, chan_dev, win_dev, samples, listing, cap, cap_rows, blocks, homes, partners = dims
    chips = win_count // 2
    pairs = blocks * homes * partners
    share_rows = pairs // win_count
    rounds = chips.bit_length() - 1
    sums, sums_out, fold_in = fold_refs[:rounds], fold_refs[rounds : 2 * rounds], fold_refs[2 * rounds :]
    pad_rows = last_in.shape[2]
    quarter, half, eighth = samples // 4, samples // 2, samples // 8
    group = lax.axis_index("chan")
    win = lax.axis_index("win")
    chip, core = win // 2, win % 2

    loads = [
        pltpu.make_async_copy(src, dst, load_sem.at[i])
        for i, (src, dst) in enumerate(
            (
                (traces_hbm, traces),
                (fwd_even_hbm, fwd_even),
                (fwd_odd_hbm, fwd_odd),
                (band_hbm, band),
                (inv_even_hbm, inv_even),
                (inv_odd_hbm, inv_odd),
                (needed_hbm, needed_ref),
                (home_hbm, home_ref),
                (partner_hbm, partner_ref),
            )
        )
    ]
    for i in (6, 7, 8, 0, 1, 2, 3, 4, 5):
        loads[i].start()

    barrier = pltpu.get_barrier_semaphore()
    cores = (core, 1 - core)
    list_peers = [(d, s) for s in range(2) for d in range(groups) if d or s]
    bits = [(chip // 2**t) % 2 for t in range(rounds)]
    partner_chips = [chip + 2**t * (1 - 2 * bits[t]) for t in range(rounds)]
    place_of = [int(format(z, f"0{rounds}b")[::-1], 2) for z in range(chips)]

    def list_id(d, s):
        return {"chan": lax.rem(group + d, groups), "win": chip * 2 + cores[s]}

    def chip_id(t, s):
        return {"win": partner_chips[t] * 2 + cores[s]}

    greeted = [list_id(d, s) for d, s in list_peers]
    greeted += [chip_id(t, 0) for t in range(rounds)] + [chip_id(rounds - 1, 1)]
    for peer in greeted:
        pl.semaphore_signal(barrier, inc=1, device_id=peer, device_id_type=MESH)

    lanes = win_dev * chan_dev
    lane = lax.broadcasted_iota(jnp.int32, (1, lanes), 1)
    lane_win = sum([(lane >= w * chan_dev).astype(jnp.int32) for w in range(1, win_dev)])
    lane_chan = lane - lane_win * chan_dev
    first_mine = group * chan_dev
    place = lax.broadcasted_iota(jnp.int32, (listing, lanes), 0)
    out_row = lax.broadcasted_iota(jnp.int32, (cap_rows, lanes), 0)
    for i in (6, 7, 8):
        loads[i].wait()
    choose = []
    for d in range(groups):
        owner = lax.rem(group + d, groups)
        column = as_column(needed_ref[pl.ds(owner, 1), :])
        hit = column == (lane_chan + first_mine)
        found = jnp.sum(jnp.where(hit, place + 1, 0), axis=0, keepdims=True)
        begin = jnp.sum((column < first_mine).astype(jnp.int32), axis=0, keepdims=True)
        target = jnp.where(found > 0, found - 1 - begin + lane_win * cap, -1)
        choose.append(jnp.where(out_row == target, 1.0, 0.0))
    choose = jnp.concatenate(choose, axis=0).astype(jnp.bfloat16)

    loads[0].wait()
    tiles = samples // 128
    rows = jnp.concatenate(
        [
            jnp.concatenate(
                [
                    traces[pl.ds(t * win_dev + w, chan_dev, stride=tiles * win_dev), :]
                    for t in range(tiles)
                ],
                axis=1,
            )
            for w in range(win_dev)
        ],
        axis=0,
    )
    count = rows.shape[0]
    folded = rows[:, :half] + rows[:, half:]
    odd_in = rows[:, :half] - rows[:, half:]
    even_in = (folded[:, :quarter] + folded[:, quarter:], folded[:, :quarter] - folded[:, quarter:])

    def transform(value, high_table, low_table):
        high, low = halves(value)
        both = dot(jnp.concatenate([high, low], axis=0), high_table)
        return both[:count] + both[count:] + dot(high, low_table)

    loads[1].wait()
    spectra = [
        transform(even_in[0], fwd_even[0], fwd_even[1]),
        transform(even_in[1], fwd_even[2], fwd_even[3]),
    ]
    loads[2].wait()
    odd_out = transform(odd_in, fwd_odd[0], fwd_odd[1])
    spectra += [odd_out[:, :quarter], odd_out[:, quarter:]]
    power = jnp.concatenate([s[:, :eighth] ** 2 + s[:, eighth:] ** 2 for s in spectra], axis=1)
    loads[3].wait()
    both = dot(jnp.concatenate(halves(power), axis=0), band[...])
    spot = lax.broadcasted_iota(jnp.int32, (1, half), 1)
    bins = jnp.where(
        spot < eighth,
        spot * 4,
        jnp.where(spot < quarter, (spot - eighth) * 4 + 2, (spot - quarter) * 2 + 1),
    )
    members = jnp.minimum(bins + BAND_REACH, half - 1) - jnp.maximum(bins - BAND_REACH, 0) + 1
    smooth = (both[:count] + both[count:]) * (1.0 / members.astype(jnp.float32))
    factor = lax.rsqrt(smooth + 1e-05)

    pl.semaphore_wait(barrier, len(greeted))

    list_copies = []
    for h in range(2):
        for k in (h, 2 + h):
            scale = factor[:, k * eighth : (k + 1) * eighth]
            whitened = jnp.concatenate(
                [spectra[k][:, :eighth] * scale, spectra[k][:, eighth:] * scale], axis=1
            ).astype(jnp.bfloat16)
            chosen = dot(choose, whitened).astype(jnp.bfloat16)
            for d in range(groups):
                listed_out[k, d] = chosen[d * cap_rows : (d + 1) * cap_rows]
        copies = []
        for n, (d, s) in enumerate(list_peers):
            copies.append(
                pltpu.make_async_remote_copy(
                    src_ref=listed_out.at[cores[s] * 2 + h, d],
                    dst_ref=listed_in.at[h, s, d],
                    send_sem=list_send.at[h, n],
                    recv_sem=list_recv.at[h, n],
                    device_id=list_id(d, s),
                    device_id_type=MESH,
                )
            )
            copies[-1].start()
        list_copies.append(copies)
        listed_in[h, 0, 0] = listed_out[core * 2 + h, 0]

    mine = needed_ref[pl.ds(group, 1), :]
    arrived = lax.broadcasted_iota(jnp.int32, (1, groups * cap_rows), 1)
    code = jnp.full((1, groups * cap_rows), -1, jnp.int32)
    for d in range(groups):
        source = lax.rem(group + groups - d, groups)
        begin = jnp.sum(
            (mine < source * chan_dev).astype(jnp.int32), axis=1, keepdims=True
        )
        for w in range(win_dev):
            low = d * cap_rows + w * cap
            within = (arrived >= low) & (arrived < low + cap)
            code = jnp.where(within, arrived - low + begin + w * listing, code)
    wanted = [as_column(partner_ref[b : b + 1, :]) for b in range(blocks)]
    wanted += [as_column(home_ref[b : b + 1, :]) for b in range(blocks)]
    wanted = jnp.concatenate(wanted, axis=0)
    per_win = blocks * (homes + partners)
    wanted = jnp.concatenate([wanted + w * listing for w in range(win_dev)], axis=0)
    pick = jnp.where(wanted == code, 1.0, 0.0).astype(jnp.bfloat16)

    def fold_copy(h, t):
        size = chips >> t + 1
        return pltpu.make_async_remote_copy(
            src_ref=sums_out[t].at[h, pl.ds((1 - bits[t]) * size, size)],
            dst_ref=fold_in[t].at[h],
            send_sem=fold_send.at[h, t],
            recv_sem=fold_recv.at[h, t],
            device_id=chip_id(t, 0),
            device_id_type=MESH,
        )

    def last_copies(h):
        bit, held = bits[-1], sums_out[-1]
        plan = (
            (held.at[h, 1 - bit, core], chip_id(rounds - 1, 0)),
            (held.at[h, 1 - bit, 1 - core], chip_id(rounds - 1, 1)),
            (held.at[h, bit, 1 - core], list_id(0, 1)),
        )
        return [
            pltpu.make_async_remote_copy(
                src_ref=src,
                dst_ref=last_in.at[h, n],
                send_sem=last_send.at[h, n],
                recv_sem=last_recv.at[h, n],
                device_id=peer,
                device_id_type=MESH,
            )
            for n, (src, peer) in enumerate(plan)
        ]

    copies_of = {(h, t): [fold_copy(h, t)] for h in range(2) for t in range(rounds - 1)}
    copies_of |= {(h, rounds - 1): last_copies(h) for h in range(2)}

    def start(h, t):
        for copy in copies_of[h, t]:
            copy.start()

    piece = min(partners, share_rows)
    for h in range(2):
        for copy in list_copies[h]:
            copy.wait_recv()
        tables = [dot(pick, listed_in[h, s].reshape(groups * cap_rows, quarter)) for s in range(2)]
        for b in range(blocks):
            for i in range(homes):
                real = imag = None
                for table in tables:
                    for w in range(win_dev):
                        at = w * per_win + blocks * partners + b * homes + i
                        home_re = table[at : at + 1, :eighth]
                        home_im = table[at : at + 1, eighth:]
                        at = w * per_win + b * partners
                        part_re = table[at : at + partners, :eighth]
                        part_im = table[at : at + partners, eighth:]
                        add_re = home_re * part_re + home_im * part_im
                        add_im = home_im * part_re - home_re * part_im
                        real = add_re if real is None else real + add_re
                        imag = add_im if imag is None else imag + add_im
                term = jnp.concatenate([real, imag], axis=1)
                for j in range(0, partners, piece):
                    row = (b * homes + i) * partners + j
                    owner, inner = row // share_rows, row % share_rows
                    at = (h, place_of[owner // 2], owner % 2, pl.ds(inner, piece))
                    sums[0][at] = term[j : j + piece]
                    sums_out[0][at] = term[j : j + piece].astype(jnp.bfloat16)
        start(h, 0)

    for t in range(rounds - 1):
        size = chips >> t + 1
        for h in range(2):
            copies_of[h, t][0].wait_recv()
            total = sums[t][h, pl.ds(bits[t] * size, size)] + fold_in[t][h].astype(jnp.float32)
            sums[t + 1][h] = total
            sums_out[t + 1][h] = total.astype(jnp.bfloat16)
            start(h, t + 1)

    loads[4].wait()
    loads[5].wait()
    for copies in list_copies:
        for copy in copies:
            copy.wait_send()
    parts = [None] * 4
    for h in range(2):
        for copy in copies_of[h, rounds - 1]:
            copy.wait_recv()
        got = [last_in[h, n].astype(jnp.float32) for n in range(3)]
        total = [sums[-1][h, bits[-1], core] + got[0], got[1] + got[2]]
        for k, value in (
            (h, jnp.where(core == 0, total[0], total[1])),
            (2 + h, jnp.where(core == 0, total[1], total[0])),
        ):
            table = inv_even[h] if k < 2 else inv_odd[h]
            both = dot(jnp.concatenate(halves(value), axis=0), table)
            parts[k] = both[:pad_rows] + both[pad_rows:]
    for copies in copies_of.values():
        for copy in copies:
            copy.wait_send()
    even = jnp.concatenate([parts[0] + parts[1], parts[0] - parts[1]], axis=1)
    odd = parts[2] + parts[3]
    norm = 1.0 / math.sqrt(samples * win_dev * win_count)
    row = win * share_rows + lax.broadcasted_iota(jnp.int32, (pad_rows, 1), 0)
    norm = jnp.where(row < live_ref[0] * (homes * partners), norm, 0.0)
    out_ref[:, :half] = ((even - odd) * norm)[:share_rows]
    out_ref[:, half:] = ((even + odd) * norm)[:share_rows]


def body(traces, needed, home_slot, partner_slot, live_blocks):
    chan_dev, win_dev, samples = traces.shape
    groups, win_count = lax.axis_size("chan"), lax.axis_size("win")
    listing = needed.shape[1]
    cap = 2 * listing // groups
    cap_rows = -(-win_dev * cap // 16) * 16
    blocks, homes = home_slot.shape
    partners = partner_slot.shape[1]
    chips = win_count // 2
    rounds = chips.bit_length() - 1
    share_rows = blocks * homes * partners // win_count
    pad_rows = max(share_rows, 16)
    quarter = samples // 4
    fwd_even, fwd_odd, band, inv_even, inv_odd = tables(samples)
    dims = (groups, win_count, chan_dev, win_dev, samples, listing, cap, cap_rows, blocks, homes, partners)
    tiled = traces.reshape(chan_dev, win_dev, samples // 128, 128).transpose(0, 2, 1, 3)
    tiled = tiled.reshape(-1, 128)
    vmem = pl.BlockSpec(memory_space=pltpu.VMEM)
    smem = pl.BlockSpec(memory_space=pltpu.SMEM)
    hbm = pl.BlockSpec(memory_space=pltpu.HBM)
    bf16, f32 = jnp.bfloat16, jnp.float32
    return pl.pallas_call(
        functools.partial(kernel, dims),
        out_shape=jax.ShapeDtypeStruct((share_rows, samples), f32),
        in_specs=[hbm] * 4 + [smem] + [hbm] * 5,
        out_specs=vmem,
        scratch_shapes=[
            pltpu.VMEM(needed.shape, jnp.int32),
            pltpu.VMEM(home_slot.shape, jnp.int32),
            pltpu.VMEM(partner_slot.shape, jnp.int32),
            pltpu.VMEM(tiled.shape, f32),
            pltpu.VMEM(fwd_even.shape, bf16),
            pltpu.VMEM(fwd_odd.shape, bf16),
            pltpu.VMEM(band.shape, bf16),
            pltpu.VMEM(inv_even.shape, bf16),
            pltpu.VMEM(inv_odd.shape, bf16),
            pltpu.VMEM((4, groups, cap_rows, quarter), bf16),
            pltpu.VMEM((2, 2, groups, cap_rows, quarter), bf16),
            pltpu.VMEM((2, 3, pad_rows, quarter), bf16),
            pltpu.SemaphoreType.DMA((9,)),
            pltpu.SemaphoreType.DMA((2, 2 * groups - 1)),
            pltpu.SemaphoreType.DMA((2, 2 * groups - 1)),
            pltpu.SemaphoreType.DMA((2, rounds)),
            pltpu.SemaphoreType.DMA((2, rounds)),
            pltpu.SemaphoreType.DMA((2, 3)),
            pltpu.SemaphoreType.DMA((2, 3)),
        ]
        + [pltpu.VMEM((2, chips >> t, 2, pad_rows, quarter), f32) for t in range(rounds)]
        + [pltpu.VMEM((2, chips >> t, 2, pad_rows, quarter), bf16) for t in range(rounds)]
        + [pltpu.VMEM((2, chips >> t + 1, 2, pad_rows, quarter), bf16) for t in range(rounds - 1)],
        compiler_params=pltpu.CompilerParams(
            collective_id=0, has_side_effects=True, vmem_limit_bytes=64 * 1024 * 1024
        ),
        cost_estimate=pl.CostEstimate(
            flops=2_000_000_000, bytes_accessed=4_000_000, transcendentals=100_000
        ),
        name="whiten_cross_stack",
    )(
        tiled,
        needed,
        home_slot,
        partner_slot,
        live_blocks,
        jnp.asarray(fwd_even),
        jnp.asarray(fwd_odd),
        jnp.asarray(band),
        jnp.asarray(inv_even),
        jnp.asarray(inv_odd),
    )


def solution(mesh):
    placed = (P("chan", "win", None), P(), P("chan", None), P("chan", None), P("chan"))
    return jax.shard_map(
        body, mesh=mesh, in_specs=placed, out_specs=P(("chan", "win"), None), check_vma=False
    )
```

```python
import functools
import math

import jax
import jax.numpy as jnp
import ml_dtypes
import numpy as np
from jax import lax
from jax.experimental import pallas as pl
from jax.experimental.pallas import tpu as pltpu
from jax.sharding import PartitionSpec as P

MESH = pl.DeviceIdType.MESH
BAND_REACH = 64


def split_table(table):
    high = table.astype(np.float32).astype(ml_dtypes.bfloat16)
    low = (table - high.astype(np.float64)).astype(np.float32).astype(ml_dtypes.bfloat16)
    return high, low


@functools.lru_cache(maxsize=None)
def tables(samples):
    quarter, half = samples // 4, samples // 2
    eighth = samples // 8
    bins_a = np.arange(0, half, 4)
    bins_b = np.arange(2, half, 4)
    bins_o = np.arange(1, half, 2)

    def forward(length, bins):
        phase = (np.arange(length)[:, None] * bins[None, :] % samples) * (2.0 * np.pi / samples)
        return np.cos(phase), -np.sin(phase)

    def inverse(length, bins):
        phase = (bins[:, None] * np.arange(length)[None, :] % samples) * (2.0 * np.pi / samples)
        weight = np.where(bins == 0, 1.0, 2.0)[:, None]
        return weight * np.cos(phase), -weight * np.sin(phase)

    odd_cos, odd_sin = forward(half, bins_o)
    fwd_a = np.concatenate(forward(quarter, bins_a), axis=1)
    fwd_b = np.concatenate(forward(quarter, bins_b), axis=1)
    fwd_o = np.concatenate(
        [odd_cos[:, :eighth], odd_sin[:, :eighth], odd_cos[:, eighth:], odd_sin[:, eighth:]], axis=1
    )
    fwd_even = np.stack([x for t in (fwd_a, fwd_b) for x in split_table(t)])
    fwd_odd = np.stack(split_table(fwd_o))
    order = np.concatenate([bins_a, bins_b, bins_o])
    inside = np.abs(order[:, None] - order[None, :]) <= BAND_REACH
    band = inside.astype(np.float32).astype(ml_dtypes.bfloat16)
    inv_cos, inv_sin = inverse(half, bins_o)
    inv_even = np.stack(
        [
            split_table(np.concatenate(inverse(quarter, bins), axis=0))[0]
            for bins in (bins_a, bins_b)
        ]
    )
    inv_odd = np.stack(
        [
            split_table(np.concatenate([inv_cos[rows], inv_sin[rows]], axis=0))[0]
            for rows in (slice(0, eighth), slice(eighth, None))
        ]
    )
    return fwd_even, fwd_odd, band, inv_even, inv_odd


def dot(left, right):
    return jnp.dot(left, right, preferred_element_type=jnp.float32)


def halves(value):
    high = value.astype(jnp.bfloat16)
    low = (value - high.astype(jnp.float32)).astype(jnp.bfloat16)
    return high, low


def as_column(row):
    n = row.shape[1]
    eye = lax.broadcasted_iota(jnp.int32, (n, n), 0) == lax.broadcasted_iota(jnp.int32, (n, n), 1)
    return jnp.sum(jnp.where(eye, jnp.broadcast_to(row, (n, n)), 0), axis=1, keepdims=True)


def kernel(
    dims,
    traces_hbm,
    needed_hbm,
    home_hbm,
    partner_hbm,
    live_ref,
    fwd_even_hbm,
    fwd_odd_hbm,
    band_hbm,
    inv_even_hbm,
    inv_odd_hbm,
    out_ref,
    needed_ref,
    home_ref,
    partner_ref,
    traces,
    fwd_even,
    fwd_odd,
    band,
    inv_even,
    inv_odd,
    listed_out,
    listed_in,
    terms,
    terms_out,
    terms_in,
    load_sem,
    list_send,
    list_recv,
    term_send,
    term_recv,
):
    groups, win_count, chan_dev, win_dev, samples, listing, cap, cap_rows, blocks, homes, partners = dims
    chips = win_count // 2
    pairs = blocks * homes * partners
    share_rows = pairs // win_count
    pad_rows = terms.shape[2]
    quarter, half, eighth = samples // 4, samples // 2, samples // 8
    group = lax.axis_index("chan")
    win = lax.axis_index("win")
    chip, core = win // 2, win % 2

    loads = [
        pltpu.make_async_copy(src, dst, load_sem.at[i])
        for i, (src, dst) in enumerate(
            (
                (traces_hbm, traces),
                (fwd_even_hbm, fwd_even),
                (fwd_odd_hbm, fwd_odd),
                (band_hbm, band),
                (inv_even_hbm, inv_even),
                (inv_odd_hbm, inv_odd),
                (needed_hbm, needed_ref),
                (home_hbm, home_ref),
                (partner_hbm, partner_ref),
            )
        )
    ]
    for i in (6, 7, 8, 0, 1, 2, 3, 4, 5):
        loads[i].start()

    barrier = pltpu.get_barrier_semaphore()
    cores = (core, 1 - core)
    list_peers = [(d, s) for s in range(2) for d in range(groups) if d or s]
    term_peers = [(d, s) for d in reversed(range(chips)) for s in range(2) if d or s]

    def list_id(d, s):
        return {"chan": lax.rem(group + d, groups), "win": chip * 2 + cores[s]}

    def term_index(d, s):
        return lax.rem(chip + d, chips) * 2 + cores[s]

    greeted = [list_id(d, s) for d, s in list_peers]
    greeted += [{"win": term_index(d, s)} for d, s in term_peers if d]
    for peer in greeted:
        pl.semaphore_signal(barrier, inc=1, device_id=peer, device_id_type=MESH)

    lanes = win_dev * chan_dev
    lane = lax.broadcasted_iota(jnp.int32, (1, lanes), 1)
    lane_win = sum([(lane >= w * chan_dev).astype(jnp.int32) for w in range(1, win_dev)])
    lane_chan = lane - lane_win * chan_dev
    first_mine = group * chan_dev
    place = lax.broadcasted_iota(jnp.int32, (listing, lanes), 0)
    out_row = lax.broadcasted_iota(jnp.int32, (cap_rows, lanes), 0)
    for i in (6, 7, 8, 0, 1, 2, 3):
        loads[i].wait()
    choose = []
    for d in range(groups):
        owner = lax.rem(group + d, groups)
        column = as_column(needed_ref[pl.ds(owner, 1), :])
        hit = column == (lane_chan + first_mine)
        found = jnp.sum(jnp.where(hit, place + 1, 0), axis=0, keepdims=True)
        begin = jnp.sum((column < first_mine).astype(jnp.int32), axis=0, keepdims=True)
        target = jnp.where(found > 0, found - 1 - begin + lane_win * cap, -1)
        choose.append(jnp.where(out_row == target, 1.0, 0.0))
    choose = jnp.concatenate(choose, axis=0).astype(jnp.bfloat16)

    tiles = samples // 128
    rows = jnp.concatenate(
        [
            jnp.concatenate(
                [
                    traces[pl.ds(t * win_dev + w, chan_dev, stride=tiles * win_dev), :]
                    for t in range(tiles)
                ],
                axis=1,
            )
            for w in range(win_dev)
        ],
        axis=0,
    )
    count = rows.shape[0]
    folded = rows[:, :half] + rows[:, half:]
    odd_in = rows[:, :half] - rows[:, half:]
    even_in = (folded[:, :quarter] + folded[:, quarter:], folded[:, :quarter] - folded[:, quarter:])

    def transform(value, high_table, low_table):
        high, low = halves(value)
        both = dot(jnp.concatenate([high, low], axis=0), high_table)
        return both[:count] + both[count:] + dot(high, low_table)

    spectra = [
        transform(even_in[0], fwd_even[0], fwd_even[1]),
        transform(even_in[1], fwd_even[2], fwd_even[3]),
    ]
    odd_out = transform(odd_in, fwd_odd[0], fwd_odd[1])
    spectra += [odd_out[:, :quarter], odd_out[:, quarter:]]
    power = jnp.concatenate([s[:, :eighth] ** 2 + s[:, eighth:] ** 2 for s in spectra], axis=1)
    both = dot(jnp.concatenate(halves(power), axis=0), band[...])
    spot = lax.broadcasted_iota(jnp.int32, (1, half), 1)
    bins = jnp.where(
        spot < eighth,
        spot * 4,
        jnp.where(spot < quarter, (spot - eighth) * 4 + 2, (spot - quarter) * 2 + 1),
    )
    members = jnp.minimum(bins + BAND_REACH, half - 1) - jnp.maximum(bins - BAND_REACH, 0) + 1
    smooth = (both[:count] + both[count:]) * (1.0 / members.astype(jnp.float32))
    factor = lax.rsqrt(smooth + 1e-05)

    list_copies = []
    for h in range(2):
        for k in (h, 2 + h):
            scale = factor[:, k * eighth : (k + 1) * eighth]
            whitened = jnp.concatenate(
                [spectra[k][:, :eighth] * scale, spectra[k][:, eighth:] * scale], axis=1
            ).astype(jnp.bfloat16)
            chosen = dot(choose, whitened).astype(jnp.bfloat16)
            for d in range(groups):
                listed_out[k, d] = chosen[d * cap_rows : (d + 1) * cap_rows]
        if h == 0:
            pl.semaphore_wait(barrier, len(greeted))
        copies = []
        for n, (d, s) in enumerate(list_peers):
            copies.append(
                pltpu.make_async_remote_copy(
                    src_ref=listed_out.at[cores[s] * 2 + h, d],
                    dst_ref=listed_in.at[h, s, d],
                    send_sem=list_send.at[h, n],
                    recv_sem=list_recv.at[h, n],
                    device_id=list_id(d, s),
                    device_id_type=MESH,
                )
            )
            copies[-1].start()
        list_copies.append(copies)
        listed_in[h, 0, 0] = listed_out[core * 2 + h, 0]

    mine = needed_ref[pl.ds(group, 1), :]
    arrived = lax.broadcasted_iota(jnp.int32, (1, groups * cap_rows), 1)
    code = jnp.full((1, groups * cap_rows), -1, jnp.int32)
    for d in range(groups):
        source = lax.rem(group + groups - d, groups)
        begin = jnp.sum(
            (mine < source * chan_dev).astype(jnp.int32), axis=1, keepdims=True
        )
        for w in range(win_dev):
            low = d * cap_rows + w * cap
            within = (arrived >= low) & (arrived < low + cap)
            code = jnp.where(within, arrived - low + begin + w * listing, code)
    wanted = [as_column(partner_ref[b : b + 1, :]) for b in range(blocks)]
    wanted += [as_column(home_ref[b : b + 1, :]) for b in range(blocks)]
    wanted = jnp.concatenate(wanted, axis=0)
    per_win = blocks * (homes + partners)
    wanted = jnp.concatenate([wanted + w * listing for w in range(win_dev)], axis=0)
    pick = jnp.where(wanted == code, 1.0, 0.0).astype(jnp.bfloat16)

    term_copies = []
    piece = min(partners, share_rows)
    for h in range(2):
        for copy in list_copies[h]:
            copy.wait_recv()
        tables = [dot(pick, listed_in[h, s].reshape(groups * cap_rows, quarter)) for s in range(2)]
        for b in range(blocks):
            for i in range(homes):
                real = imag = None
                for table in tables:
                    for w in range(win_dev):
                        at = w * per_win + blocks * partners + b * homes + i
                        home_re = table[at : at + 1, :eighth]
                        home_im = table[at : at + 1, eighth:]
                        at = w * per_win + b * partners
                        part_re = table[at : at + partners, :eighth]
                        part_im = table[at : at + partners, eighth:]
                        add_re = home_re * part_re + home_im * part_im
                        add_im = home_im * part_re - home_re * part_im
                        real = add_re if real is None else real + add_re
                        imag = add_im if imag is None else imag + add_im
                term = jnp.concatenate([real, imag], axis=1)
                for j in range(0, partners, piece):
                    row = (b * homes + i) * partners + j
                    owner, inner = row // share_rows, row % share_rows
                    terms[h, owner, inner : inner + piece, :] = term[j : j + piece]
                    terms_out[h, owner, inner : inner + piece, :] = term[j : j + piece].astype(
                        jnp.bfloat16
                    )
        copies = []
        for n, (d, s) in enumerate(term_peers):
            copies.append(
                pltpu.make_async_remote_copy(
                    src_ref=terms_out.at[h, term_index(d, s)],
                    dst_ref=terms_in.at[h, n],
                    send_sem=term_send.at[h, n],
                    recv_sem=term_recv.at[h, n],
                    device_id={"win": term_index(d, s)},
                    device_id_type=MESH,
                )
            )
            copies[-1].start()
        term_copies.append(copies)

    loads[4].wait()
    loads[5].wait()
    for copies in list_copies:
        for copy in copies:
            copy.wait_send()
    parts = [None] * 4
    for h in range(2):
        total = [terms[h, win], None]
        for n, (d, s) in enumerate(term_peers):
            term_copies[h][n].wait_recv()
            arrival = terms_in[h, n].astype(jnp.float32)
            total[s] = arrival if total[s] is None else total[s] + arrival
        for k, value in (
            (h, jnp.where(core == 0, total[0], total[1])),
            (2 + h, jnp.where(core == 0, total[1], total[0])),
        ):
            table = inv_even[h] if k < 2 else inv_odd[h]
            both = dot(jnp.concatenate(halves(value), axis=0), table)
            parts[k] = both[:pad_rows] + both[pad_rows:]
    for copies in term_copies:
        for copy in copies:
            copy.wait_send()
    even = jnp.concatenate([parts[0] + parts[1], parts[0] - parts[1]], axis=1)
    odd = parts[2] + parts[3]
    norm = 1.0 / math.sqrt(samples * win_dev * win_count)
    row = win * share_rows + lax.broadcasted_iota(jnp.int32, (pad_rows, 1), 0)
    norm = jnp.where(row < live_ref[0] * (homes * partners), norm, 0.0)
    out_ref[:, :half] = ((even - odd) * norm)[:share_rows]
    out_ref[:, half:] = ((even + odd) * norm)[:share_rows]


def body(traces, needed, home_slot, partner_slot, live_blocks):
    chan_dev, win_dev, samples = traces.shape
    groups, win_count = lax.axis_size("chan"), lax.axis_size("win")
    listing = needed.shape[1]
    cap = 2 * listing // groups
    cap_rows = -(-win_dev * cap // 16) * 16
    blocks, homes = home_slot.shape
    partners = partner_slot.shape[1]
    share_rows = blocks * homes * partners // win_count
    pad_rows = max(share_rows, 16)
    quarter = samples // 4
    fwd_even, fwd_odd, band, inv_even, inv_odd = tables(samples)
    dims = (groups, win_count, chan_dev, win_dev, samples, listing, cap, cap_rows, blocks, homes, partners)
    tiled = traces.reshape(chan_dev, win_dev, samples // 128, 128).transpose(0, 2, 1, 3)
    tiled = tiled.reshape(-1, 128)
    vmem = pl.BlockSpec(memory_space=pltpu.VMEM)
    smem = pl.BlockSpec(memory_space=pltpu.SMEM)
    hbm = pl.BlockSpec(memory_space=pltpu.HBM)
    bf16, f32 = jnp.bfloat16, jnp.float32
    return pl.pallas_call(
        functools.partial(kernel, dims),
        out_shape=jax.ShapeDtypeStruct((share_rows, samples), f32),
        in_specs=[hbm] * 4 + [smem] + [hbm] * 5,
        out_specs=vmem,
        scratch_shapes=[
            pltpu.VMEM(needed.shape, jnp.int32),
            pltpu.VMEM(home_slot.shape, jnp.int32),
            pltpu.VMEM(partner_slot.shape, jnp.int32),
            pltpu.VMEM(tiled.shape, f32),
            pltpu.VMEM(fwd_even.shape, bf16),
            pltpu.VMEM(fwd_odd.shape, bf16),
            pltpu.VMEM(band.shape, bf16),
            pltpu.VMEM(inv_even.shape, bf16),
            pltpu.VMEM(inv_odd.shape, bf16),
            pltpu.VMEM((4, groups, cap_rows, quarter), bf16),
            pltpu.VMEM((2, 2, groups, cap_rows, quarter), bf16),
            pltpu.VMEM((2, win_count, pad_rows, quarter), f32),
            pltpu.VMEM((2, win_count, pad_rows, quarter), bf16),
            pltpu.VMEM((2, win_count - 1, pad_rows, quarter), bf16),
            pltpu.SemaphoreType.DMA((9,)),
            pltpu.SemaphoreType.DMA((2, 2 * groups - 1)),
            pltpu.SemaphoreType.DMA((2, 2 * groups - 1)),
            pltpu.SemaphoreType.DMA((2, win_count - 1)),
            pltpu.SemaphoreType.DMA((2, win_count - 1)),
        ],
        compiler_params=pltpu.CompilerParams(
            collective_id=0, has_side_effects=True, vmem_limit_bytes=64 * 1024 * 1024
        ),
        cost_estimate=pl.CostEstimate(
            flops=2_000_000_000, bytes_accessed=4_000_000, transcendentals=100_000
        ),
        name="whiten_cross_stack",
    )(
        tiled,
        needed,
        home_slot,
        partner_slot,
        live_blocks,
        jnp.asarray(fwd_even),
        jnp.asarray(fwd_odd),
        jnp.asarray(band),
        jnp.asarray(inv_even),
        jnp.asarray(inv_odd),
    )


def solution(mesh):
    placed = (P("chan", "win", None), P(), P("chan", None), P("chan", None), P("chan"))
    return jax.shard_map(
        body, mesh=mesh, in_specs=placed, out_specs=P(("chan", "win"), None), check_vma=False
    )
```

```python
import functools
import math

import jax
import jax.numpy as jnp
import ml_dtypes
import numpy as np
from jax import lax
from jax.experimental import pallas as pl
from jax.experimental.pallas import tpu as pltpu
from jax.sharding import PartitionSpec as P

MESH = pl.DeviceIdType.MESH
BAND_REACH = 64


def split_table(table):
    high = table.astype(np.float32).astype(ml_dtypes.bfloat16)
    low = (table - high.astype(np.float64)).astype(np.float32).astype(ml_dtypes.bfloat16)
    return high, low


@functools.lru_cache(maxsize=None)
def tables(samples):
    quarter, half = samples // 4, samples // 2
    eighth = samples // 8
    bins_a = np.arange(0, half, 4)
    bins_b = np.arange(2, half, 4)
    bins_o = np.arange(1, half, 2)

    def forward(length, bins):
        phase = (np.arange(length)[:, None] * bins[None, :] % samples) * (2.0 * np.pi / samples)
        return np.cos(phase), -np.sin(phase)

    def inverse(length, bins):
        phase = (bins[:, None] * np.arange(length)[None, :] % samples) * (2.0 * np.pi / samples)
        weight = np.where(bins == 0, 1.0, 2.0)[:, None]
        return weight * np.cos(phase), -weight * np.sin(phase)

    odd_cos, odd_sin = forward(half, bins_o)
    fwd_a = np.concatenate(forward(quarter, bins_a), axis=1)
    fwd_b = np.concatenate(forward(quarter, bins_b), axis=1)
    fwd_o = np.concatenate(
        [odd_cos[:, :eighth], odd_sin[:, :eighth], odd_cos[:, eighth:], odd_sin[:, eighth:]], axis=1
    )
    fwd_even = np.stack([x for t in (fwd_a, fwd_b) for x in split_table(t)])
    fwd_odd = np.stack(split_table(fwd_o))
    inv_cos, inv_sin = inverse(half, bins_o)
    inv_even = np.stack(
        [
            split_table(np.concatenate(inverse(quarter, bins), axis=0))[0]
            for bins in (bins_a, bins_b)
        ]
    )
    inv_odd = np.stack(
        [
            split_table(np.concatenate([inv_cos[rows], inv_sin[rows]], axis=0))[0]
            for rows in (slice(0, eighth), slice(eighth, None))
        ]
    )
    return fwd_even, fwd_odd, inv_even, inv_odd


def dot(left, right):
    return jnp.dot(left, right, preferred_element_type=jnp.float32)


def halves(value):
    high = value.astype(jnp.bfloat16)
    low = (value - high.astype(jnp.float32)).astype(jnp.bfloat16)
    return high, low


def as_column(row):
    n = row.shape[1]
    eye = lax.broadcasted_iota(jnp.int32, (n, n), 0) == lax.broadcasted_iota(jnp.int32, (n, n), 1)
    return jnp.sum(jnp.where(eye, jnp.broadcast_to(row, (n, n)), 0), axis=1, keepdims=True)


def kernel(
    dims,
    traces_hbm,
    needed_hbm,
    home_hbm,
    partner_hbm,
    live_ref,
    fwd_even_hbm,
    fwd_odd_hbm,
    inv_even_hbm,
    inv_odd_hbm,
    out_ref,
    needed_ref,
    home_ref,
    partner_ref,
    traces,
    fwd_even,
    fwd_odd,
    inv_even,
    inv_odd,
    listed_out,
    listed_in,
    terms,
    terms_out,
    terms_in,
    load_sem,
    list_send,
    list_recv,
    term_send,
    term_recv,
):
    groups, win_count, chan_dev, win_dev, samples, listing, cap, cap_rows, blocks, homes, partners = dims
    chips = win_count // 2
    pairs = blocks * homes * partners
    share_rows = pairs // win_count
    pad_rows = terms.shape[2]
    quarter, half, eighth = samples // 4, samples // 2, samples // 8
    group = lax.axis_index("chan")
    win = lax.axis_index("win")
    chip, core = win // 2, win % 2

    loads = [
        pltpu.make_async_copy(src, dst, load_sem.at[i])
        for i, (src, dst) in enumerate(
            (
                (traces_hbm, traces),
                (fwd_even_hbm, fwd_even),
                (fwd_odd_hbm, fwd_odd),
                (inv_even_hbm, inv_even),
                (inv_odd_hbm, inv_odd),
                (needed_hbm, needed_ref),
                (home_hbm, home_ref),
                (partner_hbm, partner_ref),
            )
        )
    ]
    for i in (5, 0, 1, 2, 6, 7):
        loads[i].start()

    barrier = pltpu.get_barrier_semaphore()
    cores = (core, 1 - core)
    list_peers = [(d, s) for s in range(2) for d in range(groups) if d or s]
    term_peers = [(d, s) for d in reversed(range(chips)) for s in range(2) if d or s]

    def list_id(d, s):
        return {"chan": lax.rem(group + d, groups), "win": chip * 2 + cores[s]}

    def term_index(d, s):
        return lax.rem(chip + d, chips) * 2 + cores[s]

    greeted = [list_id(d, s) for d, s in list_peers]
    greeted += [{"win": term_index(d, s)} for d, s in term_peers if d]
    for peer in greeted:
        pl.semaphore_signal(barrier, inc=1, device_id=peer, device_id_type=MESH)

    def bins_along(shape, axis):
        spot = lax.broadcasted_iota(jnp.int32, shape, axis)
        odd_or_b = jnp.where(spot < quarter, (spot - eighth) * 4 + 2, (spot - quarter) * 2 + 1)
        return jnp.where(spot < eighth, spot * 4, odd_or_b)

    bins = bins_along((1, half), 1)
    apart = jnp.abs(bins_along((half, 1), 0) - bins)
    band = jnp.where(apart <= BAND_REACH, 1.0, 0.0).astype(jnp.bfloat16)

    lanes = win_dev * chan_dev
    lane = lax.broadcasted_iota(jnp.int32, (1, lanes), 1)
    lane_win = sum([(lane >= w * chan_dev).astype(jnp.int32) for w in range(1, win_dev)])
    lane_chan = lane - lane_win * chan_dev
    first_mine = group * chan_dev
    place = lax.broadcasted_iota(jnp.int32, (listing, lanes), 0)
    out_row = lax.broadcasted_iota(jnp.int32, (cap_rows, lanes), 0)
    loads[5].wait()
    choose = []
    for d in range(groups):
        owner = lax.rem(group + d, groups)
        column = as_column(needed_ref[pl.ds(owner, 1), :])
        hit = column == (lane_chan + first_mine)
        found = jnp.sum(jnp.where(hit, place + 1, 0), axis=0, keepdims=True)
        begin = jnp.sum((column < first_mine).astype(jnp.int32), axis=0, keepdims=True)
        target = jnp.where(found > 0, found - 1 - begin + lane_win * cap, -1)
        choose.append(jnp.where(out_row == target, 1.0, 0.0))
    choose = jnp.concatenate(choose, axis=0).astype(jnp.bfloat16)

    loads[0].wait()
    tiles = samples // 128
    rows = jnp.concatenate(
        [
            jnp.concatenate(
                [
                    traces[pl.ds(t * win_dev + w, chan_dev, stride=tiles * win_dev), :]
                    for t in range(tiles)
                ],
                axis=1,
            )
            for w in range(win_dev)
        ],
        axis=0,
    )
    count = rows.shape[0]
    folded = rows[:, :half] + rows[:, half:]
    odd_in = rows[:, :half] - rows[:, half:]
    even_in = (folded[:, :quarter] + folded[:, quarter:], folded[:, :quarter] - folded[:, quarter:])

    def transform(value, high_table, low_table):
        high, low = halves(value)
        both = dot(jnp.concatenate([high, low], axis=0), high_table)
        return both[:count] + both[count:] + dot(high, low_table)

    loads[1].wait()
    spectra = [
        transform(even_in[0], fwd_even[0], fwd_even[1]),
        transform(even_in[1], fwd_even[2], fwd_even[3]),
    ]
    loads[2].wait()
    odd_out = transform(odd_in, fwd_odd[0], fwd_odd[1])
    spectra += [odd_out[:, :quarter], odd_out[:, quarter:]]
    power = jnp.concatenate([s[:, :eighth] ** 2 + s[:, eighth:] ** 2 for s in spectra], axis=1)
    both = dot(jnp.concatenate(halves(power), axis=0), band)
    members = jnp.minimum(bins + BAND_REACH, half - 1) - jnp.maximum(bins - BAND_REACH, 0) + 1
    smooth = (both[:count] + both[count:]) * (1.0 / members.astype(jnp.float32))
    factor = lax.rsqrt(smooth + 1e-05)

    pl.semaphore_wait(barrier, len(greeted))

    list_copies = []
    for h in range(2):
        for k in (h, 2 + h):
            scale = factor[:, k * eighth : (k + 1) * eighth]
            whitened = jnp.concatenate(
                [spectra[k][:, :eighth] * scale, spectra[k][:, eighth:] * scale], axis=1
            ).astype(jnp.bfloat16)
            chosen = dot(choose, whitened).astype(jnp.bfloat16)
            for d in range(groups):
                listed_out[k, d] = chosen[d * cap_rows : (d + 1) * cap_rows]
        copies = []
        for n, (d, s) in enumerate(list_peers):
            copies.append(
                pltpu.make_async_remote_copy(
                    src_ref=listed_out.at[cores[s] * 2 + h, d],
                    dst_ref=listed_in.at[h, s, d],
                    send_sem=list_send.at[h, n],
                    recv_sem=list_recv.at[h, n],
                    device_id=list_id(d, s),
                    device_id_type=MESH,
                )
            )
            copies[-1].start()
        list_copies.append(copies)
        listed_in[h, 0, 0] = listed_out[core * 2 + h, 0]
    for i in (3, 4):
        loads[i].start()
    for i in (6, 7):
        loads[i].wait()

    mine = needed_ref[pl.ds(group, 1), :]
    arrived = lax.broadcasted_iota(jnp.int32, (1, groups * cap_rows), 1)
    code = jnp.full((1, groups * cap_rows), -1, jnp.int32)
    for d in range(groups):
        source = lax.rem(group + groups - d, groups)
        begin = jnp.sum(
            (mine < source * chan_dev).astype(jnp.int32), axis=1, keepdims=True
        )
        for w in range(win_dev):
            low = d * cap_rows + w * cap
            within = (arrived >= low) & (arrived < low + cap)
            code = jnp.where(within, arrived - low + begin + w * listing, code)
    wanted = [as_column(partner_ref[b : b + 1, :]) for b in range(blocks)]
    wanted += [as_column(home_ref[b : b + 1, :]) for b in range(blocks)]
    wanted = jnp.concatenate(wanted, axis=0)
    per_win = blocks * (homes + partners)
    wanted = jnp.concatenate([wanted + w * listing for w in range(win_dev)], axis=0)
    pick = jnp.where(wanted == code, 1.0, 0.0).astype(jnp.bfloat16)

    term_copies = []
    piece = min(partners, share_rows)
    for h in range(2):
        for copy in list_copies[h]:
            copy.wait_recv()
        tables = [dot(pick, listed_in[h, s].reshape(groups * cap_rows, quarter)) for s in range(2)]
        for b in range(blocks):
            for i in range(homes):
                real = imag = None
                for table in tables:
                    for w in range(win_dev):
                        at = w * per_win + blocks * partners + b * homes + i
                        home_re = table[at : at + 1, :eighth]
                        home_im = table[at : at + 1, eighth:]
                        at = w * per_win + b * partners
                        part_re = table[at : at + partners, :eighth]
                        part_im = table[at : at + partners, eighth:]
                        add_re = home_re * part_re + home_im * part_im
                        add_im = home_im * part_re - home_re * part_im
                        real = add_re if real is None else real + add_re
                        imag = add_im if imag is None else imag + add_im
                term = jnp.concatenate([real, imag], axis=1)
                for j in range(0, partners, piece):
                    row = (b * homes + i) * partners + j
                    owner, inner = row // share_rows, row % share_rows
                    terms[h, owner, inner : inner + piece, :] = term[j : j + piece]
                    terms_out[h, owner, inner : inner + piece, :] = term[j : j + piece].astype(
                        jnp.bfloat16
                    )
        copies = []
        for n, (d, s) in enumerate(term_peers):
            copies.append(
                pltpu.make_async_remote_copy(
                    src_ref=terms_out.at[h, term_index(d, s)],
                    dst_ref=terms_in.at[h, n],
                    send_sem=term_send.at[h, n],
                    recv_sem=term_recv.at[h, n],
                    device_id={"win": term_index(d, s)},
                    device_id_type=MESH,
                )
            )
            copies[-1].start()
        term_copies.append(copies)

    loads[3].wait()
    loads[4].wait()
    for copies in list_copies:
        for copy in copies:
            copy.wait_send()
    parts = [None] * 4
    for h in range(2):
        total = [terms[h, win], None]
        for n, (d, s) in enumerate(term_peers):
            term_copies[h][n].wait_recv()
            arrival = terms_in[h, n].astype(jnp.float32)
            total[s] = arrival if total[s] is None else total[s] + arrival
        for k, value in (
            (h, jnp.where(core == 0, total[0], total[1])),
            (2 + h, jnp.where(core == 0, total[1], total[0])),
        ):
            table = inv_even[h] if k < 2 else inv_odd[h]
            both = dot(jnp.concatenate(halves(value), axis=0), table)
            parts[k] = both[:pad_rows] + both[pad_rows:]
    for copies in term_copies:
        for copy in copies:
            copy.wait_send()
    even = jnp.concatenate([parts[0] + parts[1], parts[0] - parts[1]], axis=1)
    odd = parts[2] + parts[3]
    norm = 1.0 / math.sqrt(samples * win_dev * win_count)
    row = win * share_rows + lax.broadcasted_iota(jnp.int32, (pad_rows, 1), 0)
    norm = jnp.where(row < live_ref[0] * (homes * partners), norm, 0.0)
    out_ref[:, :half] = ((even - odd) * norm)[:share_rows]
    out_ref[:, half:] = ((even + odd) * norm)[:share_rows]


def body(traces, needed, home_slot, partner_slot, live_blocks):
    chan_dev, win_dev, samples = traces.shape
    groups, win_count = lax.axis_size("chan"), lax.axis_size("win")
    listing = needed.shape[1]
    cap = 2 * listing // groups
    cap_rows = -(-win_dev * cap // 16) * 16
    blocks, homes = home_slot.shape
    partners = partner_slot.shape[1]
    share_rows = blocks * homes * partners // win_count
    pad_rows = max(share_rows, 16)
    quarter = samples // 4
    fwd_even, fwd_odd, inv_even, inv_odd = tables(samples)
    dims = (groups, win_count, chan_dev, win_dev, samples, listing, cap, cap_rows, blocks, homes, partners)
    tiled = traces.reshape(chan_dev, win_dev, samples // 128, 128).transpose(0, 2, 1, 3)
    tiled = tiled.reshape(-1, 128)
    vmem = pl.BlockSpec(memory_space=pltpu.VMEM)
    smem = pl.BlockSpec(memory_space=pltpu.SMEM)
    hbm = pl.BlockSpec(memory_space=pltpu.HBM)
    bf16, f32 = jnp.bfloat16, jnp.float32
    return pl.pallas_call(
        functools.partial(kernel, dims),
        out_shape=jax.ShapeDtypeStruct((share_rows, samples), f32),
        in_specs=[hbm] * 4 + [smem] + [hbm] * 4,
        out_specs=vmem,
        scratch_shapes=[
            pltpu.VMEM(needed.shape, jnp.int32),
            pltpu.VMEM(home_slot.shape, jnp.int32),
            pltpu.VMEM(partner_slot.shape, jnp.int32),
            pltpu.VMEM(tiled.shape, f32),
            pltpu.VMEM(fwd_even.shape, bf16),
            pltpu.VMEM(fwd_odd.shape, bf16),
            pltpu.VMEM(inv_even.shape, bf16),
            pltpu.VMEM(inv_odd.shape, bf16),
            pltpu.VMEM((4, groups, cap_rows, quarter), bf16),
            pltpu.VMEM((2, 2, groups, cap_rows, quarter), bf16),
            pltpu.VMEM((2, win_count, pad_rows, quarter), f32),
            pltpu.VMEM((2, win_count, pad_rows, quarter), bf16),
            pltpu.VMEM((2, win_count - 1, pad_rows, quarter), bf16),
            pltpu.SemaphoreType.DMA((8,)),
            pltpu.SemaphoreType.DMA((2, 2 * groups - 1)),
            pltpu.SemaphoreType.DMA((2, 2 * groups - 1)),
            pltpu.SemaphoreType.DMA((2, win_count - 1)),
            pltpu.SemaphoreType.DMA((2, win_count - 1)),
        ],
        compiler_params=pltpu.CompilerParams(
            collective_id=0, has_side_effects=True, vmem_limit_bytes=64 * 1024 * 1024
        ),
        cost_estimate=pl.CostEstimate(
            flops=2_000_000_000, bytes_accessed=4_000_000, transcendentals=100_000
        ),
        name="whiten_cross_stack",
    )(
        tiled,
        needed,
        home_slot,
        partner_slot,
        live_blocks,
        jnp.asarray(fwd_even),
        jnp.asarray(fwd_odd),
        jnp.asarray(inv_even),
        jnp.asarray(inv_odd),
    )


def solution(mesh):
    placed = (P("chan", "win", None), P(), P("chan", None), P("chan", None), P("chan"))
    return jax.shard_map(
        body, mesh=mesh, in_specs=placed, out_specs=P(("chan", "win"), None), check_vma=False
    )
```

```python
import functools
import math

import jax
import jax.numpy as jnp
import ml_dtypes
import numpy as np
from jax import lax
from jax.experimental import pallas as pl
from jax.experimental.pallas import tpu as pltpu
from jax.sharding import PartitionSpec as P

MESH = pl.DeviceIdType.MESH
BAND_REACH = 64


def split_table(table):
    high = table.astype(np.float32).astype(ml_dtypes.bfloat16)
    low = (table - high.astype(np.float64)).astype(np.float32).astype(ml_dtypes.bfloat16)
    return high, low


@functools.lru_cache(maxsize=None)
def tables(samples):
    quarter, half = samples // 4, samples // 2
    eighth = samples // 8
    bins_a = np.arange(0, half, 4)
    bins_b = np.arange(2, half, 4)
    bins_o = np.arange(1, half, 2)

    def forward(length, bins):
        phase = (np.arange(length)[:, None] * bins[None, :] % samples) * (2.0 * np.pi / samples)
        return np.cos(phase), -np.sin(phase)

    def inverse(length, bins):
        phase = (bins[:, None] * np.arange(length)[None, :] % samples) * (2.0 * np.pi / samples)
        weight = np.where(bins == 0, 1.0, 2.0)[:, None]
        return weight * np.cos(phase), -weight * np.sin(phase)

    odd_cos, odd_sin = forward(half, bins_o)
    fwd_a = np.concatenate(forward(quarter, bins_a), axis=1)
    fwd_b = np.concatenate(forward(quarter, bins_b), axis=1)
    fwd_o = np.concatenate(
        [odd_cos[:, :eighth], odd_sin[:, :eighth], odd_cos[:, eighth:], odd_sin[:, eighth:]], axis=1
    )
    fwd_even = np.stack([x for t in (fwd_a, fwd_b) for x in split_table(t)])
    fwd_odd = np.stack(split_table(fwd_o))
    inv_cos, inv_sin = inverse(half, bins_o)
    inv_even = np.stack(
        [
            split_table(np.concatenate(inverse(quarter, bins), axis=0))[0]
            for bins in (bins_a, bins_b)
        ]
    )
    inv_odd = np.stack(
        [
            split_table(np.concatenate([inv_cos[rows], inv_sin[rows]], axis=0))[0]
            for rows in (slice(0, eighth), slice(eighth, None))
        ]
    )
    return fwd_even, fwd_odd, inv_even, inv_odd


def dot(left, right):
    return jnp.dot(left, right, preferred_element_type=jnp.float32)


def halves(value):
    high = value.astype(jnp.bfloat16)
    low = (value - high.astype(jnp.float32)).astype(jnp.bfloat16)
    return high, low


def as_column(row):
    n = row.shape[1]
    eye = lax.broadcasted_iota(jnp.int32, (n, n), 0) == lax.broadcasted_iota(jnp.int32, (n, n), 1)
    return jnp.sum(jnp.where(eye, jnp.broadcast_to(row, (n, n)), 0), axis=1, keepdims=True)


def kernel(
    dims,
    traces_hbm,
    needed_hbm,
    home_hbm,
    partner_hbm,
    live_ref,
    fwd_even_hbm,
    fwd_odd_hbm,
    inv_even_hbm,
    inv_odd_hbm,
    out_ref,
    needed_ref,
    home_ref,
    partner_ref,
    traces,
    fwd_even,
    fwd_odd,
    inv_even,
    inv_odd,
    listed_out,
    listed_in,
    terms,
    terms_out,
    terms_in,
    load_sem,
    list_send,
    list_recv,
    term_send,
    term_recv,
):
    groups, win_count, chan_dev, win_dev, samples, listing, cap, cap_rows, blocks, homes, partners = dims
    chips = win_count // 2
    pairs = blocks * homes * partners
    share_rows = pairs // win_count
    pad_rows = terms.shape[2]
    quarter, half, eighth = samples // 4, samples // 2, samples // 8
    group = lax.axis_index("chan")
    win = lax.axis_index("win")
    chip, core = win // 2, win % 2

    loads = [
        pltpu.make_async_copy(src, dst, load_sem.at[i])
        for i, (src, dst) in enumerate(
            (
                (traces_hbm, traces),
                (fwd_even_hbm, fwd_even),
                (fwd_odd_hbm, fwd_odd),
                (inv_even_hbm, inv_even),
                (inv_odd_hbm, inv_odd),
                (needed_hbm, needed_ref),
                (home_hbm, home_ref),
                (partner_hbm, partner_ref),
            )
        )
    ]
    for i in (5, 0, 1, 2, 6, 7):
        loads[i].start()

    barrier = pltpu.get_barrier_semaphore()
    cores = (core, 1 - core)
    list_peers = [(d, s) for s in range(2) for d in range(groups) if d or s]
    term_peers = [(d, s) for d in reversed(range(chips)) for s in range(2) if d or s]

    def list_id(d, s):
        return {"chan": lax.rem(group + d, groups), "win": chip * 2 + cores[s]}

    def term_index(d, s):
        return lax.rem(chip + d, chips) * 2 + cores[s]

    greeted = [list_id(d, s) for d, s in list_peers]
    greeted += [{"win": term_index(d, s)} for d, s in term_peers if d]
    for peer in greeted:
        pl.semaphore_signal(barrier, inc=1, device_id=peer, device_id_type=MESH)

    def bins_along(shape, axis):
        spot = lax.broadcasted_iota(jnp.int32, shape, axis)
        odd_or_b = jnp.where(spot < quarter, (spot - eighth) * 4 + 2, (spot - quarter) * 2 + 1)
        return jnp.where(spot < eighth, spot * 4, odd_or_b)

    bins = bins_along((1, half), 1)
    apart = jnp.abs(bins_along((half, 1), 0) - bins)
    band = jnp.where(apart <= BAND_REACH, 1.0, 0.0).astype(jnp.bfloat16)

    lanes = win_dev * chan_dev
    lane = lax.broadcasted_iota(jnp.int32, (1, lanes), 1)
    lane_win = sum([(lane >= w * chan_dev).astype(jnp.int32) for w in range(1, win_dev)])
    lane_chan = lane - lane_win * chan_dev
    first_mine = group * chan_dev
    place = lax.broadcasted_iota(jnp.int32, (listing, lanes), 0)
    out_row = lax.broadcasted_iota(jnp.int32, (cap_rows, lanes), 0)
    loads[5].wait()
    choose = []
    for d in range(groups):
        owner = lax.rem(group + d, groups)
        column = as_column(needed_ref[pl.ds(owner, 1), :])
        hit = column == (lane_chan + first_mine)
        found = jnp.sum(jnp.where(hit, place + 1, 0), axis=0, keepdims=True)
        begin = jnp.sum((column < first_mine).astype(jnp.int32), axis=0, keepdims=True)
        target = jnp.where(found > 0, found - 1 - begin + lane_win * cap, -1)
        choose.append(jnp.where(out_row == target, 1.0, 0.0))
    choose = jnp.concatenate(choose, axis=0).astype(jnp.bfloat16)

    loads[0].wait()
    tiles = samples // 128
    rows = jnp.concatenate(
        [
            jnp.concatenate(
                [
                    traces[pl.ds(t * win_dev + w, chan_dev, stride=tiles * win_dev), :]
                    for t in range(tiles)
                ],
                axis=1,
            )
            for w in range(win_dev)
        ],
        axis=0,
    )
    count = rows.shape[0]
    folded = rows[:, :half] + rows[:, half:]
    odd_in = rows[:, :half] - rows[:, half:]
    even_in = (folded[:, :quarter] + folded[:, quarter:], folded[:, :quarter] - folded[:, quarter:])

    def transform(value, high_table, low_table):
        high, low = halves(value)
        both = dot(jnp.concatenate([high, low], axis=0), high_table)
        return both[:count] + both[count:] + dot(high, low_table)

    loads[1].wait()
    spectra = [
        transform(even_in[0], fwd_even[0], fwd_even[1]),
        transform(even_in[1], fwd_even[2], fwd_even[3]),
    ]
    loads[2].wait()
    odd_out = transform(odd_in, fwd_odd[0], fwd_odd[1])
    spectra += [odd_out[:, :quarter], odd_out[:, quarter:]]
    power = jnp.concatenate([s[:, :eighth] ** 2 + s[:, eighth:] ** 2 for s in spectra], axis=1)
    both = dot(jnp.concatenate(halves(power), axis=0), band)
    members = jnp.minimum(bins + BAND_REACH, half - 1) - jnp.maximum(bins - BAND_REACH, 0) + 1
    smooth = (both[:count] + both[count:]) * (1.0 / members.astype(jnp.float32))
    factor = lax.rsqrt(smooth + 1e-05)

    pl.semaphore_wait(barrier, len(greeted))

    list_copies = []
    for h in range(2):
        for k in (h, 2 + h):
            scale = factor[:, k * eighth : (k + 1) * eighth]
            whitened = jnp.concatenate(
                [spectra[k][:, :eighth] * scale, spectra[k][:, eighth:] * scale], axis=1
            ).astype(jnp.bfloat16)
            chosen = dot(choose, whitened).astype(jnp.bfloat16)
            for d in range(groups):
                listed_out[k, d] = chosen[d * cap_rows : (d + 1) * cap_rows]
        copies = []
        for n, (d, s) in enumerate(list_peers):
            copies.append(
                pltpu.make_async_remote_copy(
                    src_ref=listed_out.at[cores[s] * 2 + h, d],
                    dst_ref=listed_in.at[h, s, d],
                    send_sem=list_send.at[h, n],
                    recv_sem=list_recv.at[h, n],
                    device_id=list_id(d, s),
                    device_id_type=MESH,
                )
            )
            copies[-1].start()
        list_copies.append(copies)
        listed_in[h, 0, 0] = listed_out[core * 2 + h, 0]
    for i in (3, 4):
        loads[i].start()
    for i in (6, 7):
        loads[i].wait()

    mine = needed_ref[pl.ds(group, 1), :]
    arrived = lax.broadcasted_iota(jnp.int32, (1, groups * cap_rows), 1)
    code = jnp.full((1, groups * cap_rows), -1, jnp.int32)
    for d in range(groups):
        source = lax.rem(group + groups - d, groups)
        begin = jnp.sum(
            (mine < source * chan_dev).astype(jnp.int32), axis=1, keepdims=True
        )
        for w in range(win_dev):
            low = d * cap_rows + w * cap
            within = (arrived >= low) & (arrived < low + cap)
            code = jnp.where(within, arrived - low + begin + w * listing, code)
    wanted = [as_column(partner_ref[b : b + 1, :]) for b in range(blocks)]
    wanted += [as_column(home_ref[b : b + 1, :]) for b in range(blocks)]
    wanted = jnp.concatenate(wanted, axis=0)
    per_win = blocks * (homes + partners)
    wanted = jnp.concatenate([wanted + w * listing for w in range(win_dev)], axis=0)
    pick = jnp.where(wanted == code, 1.0, 0.0).astype(jnp.bfloat16)

    term_copies = []
    piece = min(partners, share_rows)
    for h in range(2):
        for copy in list_copies[h]:
            copy.wait_recv()
        tables = [dot(pick, listed_in[h, s].reshape(groups * cap_rows, quarter)) for s in range(2)]
        for b in range(blocks):
            for i in range(homes):
                real = imag = None
                for table in tables:
                    for w in range(win_dev):
                        at = w * per_win + blocks * partners + b * homes + i
                        home_re = table[at : at + 1, :eighth]
                        home_im = table[at : at + 1, eighth:]
                        at = w * per_win + b * partners
                        part_re = table[at : at + partners, :eighth]
                        part_im = table[at : at + partners, eighth:]
                        add_re = home_re * part_re + home_im * part_im
                        add_im = home_im * part_re - home_re * part_im
                        real = add_re if real is None else real + add_re
                        imag = add_im if imag is None else imag + add_im
                term = jnp.concatenate([real, imag], axis=1)
                for j in range(0, partners, piece):
                    row = (b * homes + i) * partners + j
                    owner, inner = row // share_rows, row % share_rows
                    terms[h, owner, inner : inner + piece, :] = term[j : j + piece]
                    terms_out[h, owner, inner : inner + piece, :] = term[j : j + piece].astype(
                        jnp.bfloat16
                    )
        copies = []
        for n, (d, s) in enumerate(term_peers):
            copies.append(
                pltpu.make_async_remote_copy(
                    src_ref=terms_out.at[h, term_index(d, s)],
                    dst_ref=terms_in.at[h, n],
                    send_sem=term_send.at[h, n],
                    recv_sem=term_recv.at[h, n],
                    device_id={"win": term_index(d, s)},
                    device_id_type=MESH,
                )
            )
            copies[-1].start()
        term_copies.append(copies)

    loads[3].wait()
    loads[4].wait()
    for copies in list_copies:
        for copy in copies:
            copy.wait_send()
    parts = [None] * 4
    for h in range(2):
        total = [terms[h, win], None]
        for n, (d, s) in enumerate(term_peers):
            term_copies[h][n].wait_recv()
            arrival = terms_in[h, n].astype(jnp.float32)
            total[s] = arrival if total[s] is None else total[s] + arrival
        for k, value in (
            (h, jnp.where(core == 0, total[0], total[1])),
            (2 + h, jnp.where(core == 0, total[1], total[0])),
        ):
            table = inv_even[h] if k < 2 else inv_odd[h]
            both = dot(jnp.concatenate(halves(value), axis=0), table)
            parts[k] = both[:pad_rows] + both[pad_rows:]
    for copies in term_copies:
        for copy in copies:
            copy.wait_send()
    even = jnp.concatenate([parts[0] + parts[1], parts[0] - parts[1]], axis=1)
    odd = parts[2] + parts[3]
    norm = 1.0 / math.sqrt(samples * win_dev * win_count)
    row = win * share_rows + lax.broadcasted_iota(jnp.int32, (pad_rows, 1), 0)
    norm = jnp.where(row < live_ref[0] * (homes * partners), norm, 0.0)
    out_ref[:, :half] = ((even - odd) * norm)[:share_rows]
    out_ref[:, half:] = ((even + odd) * norm)[:share_rows]


def hand_over(held, out, sems):
    copies = [
        pltpu.make_async_copy(held.at[pl.ds(at, 8)], out.at[pl.ds(at, 8)], sems.at[at // 8])
        for at in range(0, held.shape[0], 8)
    ]
    for copy in copies:
        copy.start()
    for copy in copies:
        copy.wait()


def body(traces, needed, home_slot, partner_slot, live_blocks):
    chan_dev, win_dev, samples = traces.shape
    groups, win_count = lax.axis_size("chan"), lax.axis_size("win")
    listing = needed.shape[1]
    cap = 2 * listing // groups
    cap_rows = -(-win_dev * cap // 16) * 16
    blocks, homes = home_slot.shape
    partners = partner_slot.shape[1]
    share_rows = blocks * homes * partners // win_count
    pad_rows = max(share_rows, 16)
    quarter = samples // 4
    fwd_even, fwd_odd, inv_even, inv_odd = tables(samples)
    dims = (groups, win_count, chan_dev, win_dev, samples, listing, cap, cap_rows, blocks, homes, partners)
    tiled = traces.reshape(chan_dev, win_dev, samples // 128, 128).transpose(0, 2, 1, 3)
    tiled = tiled.reshape(-1, 128)
    vmem = pl.BlockSpec(memory_space=pltpu.VMEM)
    smem = pl.BlockSpec(memory_space=pltpu.SMEM)
    hbm = pl.BlockSpec(memory_space=pltpu.HBM)
    bf16, f32 = jnp.bfloat16, jnp.float32
    stacked = pl.pallas_call(
        functools.partial(kernel, dims),
        out_shape=jax.ShapeDtypeStruct((share_rows, samples), f32),
        in_specs=[hbm] * 4 + [smem] + [hbm] * 4,
        out_specs=vmem,
        scratch_shapes=[
            pltpu.VMEM(needed.shape, jnp.int32),
            pltpu.VMEM(home_slot.shape, jnp.int32),
            pltpu.VMEM(partner_slot.shape, jnp.int32),
            pltpu.VMEM(tiled.shape, f32),
            pltpu.VMEM(fwd_even.shape, bf16),
            pltpu.VMEM(fwd_odd.shape, bf16),
            pltpu.VMEM(inv_even.shape, bf16),
            pltpu.VMEM(inv_odd.shape, bf16),
            pltpu.VMEM((4, groups, cap_rows, quarter), bf16),
            pltpu.VMEM((2, 2, groups, cap_rows, quarter), bf16),
            pltpu.VMEM((2, win_count, pad_rows, quarter), f32),
            pltpu.VMEM((2, win_count, pad_rows, quarter), bf16),
            pltpu.VMEM((2, win_count - 1, pad_rows, quarter), bf16),
            pltpu.SemaphoreType.DMA((8,)),
            pltpu.SemaphoreType.DMA((2, 2 * groups - 1)),
            pltpu.SemaphoreType.DMA((2, 2 * groups - 1)),
            pltpu.SemaphoreType.DMA((2, win_count - 1)),
            pltpu.SemaphoreType.DMA((2, win_count - 1)),
        ],
        compiler_params=pltpu.CompilerParams(
            collective_id=0, has_side_effects=True, vmem_limit_bytes=64 * 1024 * 1024
        ),
        cost_estimate=pl.CostEstimate(
            flops=2_000_000_000, bytes_accessed=4_000_000, transcendentals=100_000
        ),
        name="whiten_cross_stack",
    )(
        tiled,
        needed,
        home_slot,
        partner_slot,
        live_blocks,
        jnp.asarray(fwd_even),
        jnp.asarray(fwd_odd),
        jnp.asarray(inv_even),
        jnp.asarray(inv_odd),
    )
    return pl.pallas_call(
        hand_over,
        out_shape=jax.ShapeDtypeStruct(stacked.shape, f32),
        in_specs=[hbm],
        out_specs=hbm,
        scratch_shapes=[pltpu.SemaphoreType.DMA((share_rows // 8,))],
        compiler_params=pltpu.CompilerParams(vmem_limit_bytes=64 * 1024 * 1024),
        name="hand_over",
    )(stacked)


def solution(mesh):
    placed = (P("chan", "win", None), P(), P("chan", None), P("chan", None), P("chan"))
    return jax.shard_map(
        body, mesh=mesh, in_specs=placed, out_specs=P(("chan", "win"), None), check_vma=False
    )
```

```python
import functools
import math

import jax
import jax.numpy as jnp
import ml_dtypes
import numpy as np
from jax import lax
from jax.experimental import pallas as pl
from jax.experimental.pallas import tpu as pltpu
from jax.sharding import PartitionSpec as P

MESH = pl.DeviceIdType.MESH
BAND_REACH = 64


def split_table(table):
    high = table.astype(np.float32).astype(ml_dtypes.bfloat16)
    low = (table - high.astype(np.float64)).astype(np.float32).astype(ml_dtypes.bfloat16)
    return high, low


@functools.lru_cache(maxsize=None)
def tables(samples):
    quarter, half = samples // 4, samples // 2
    eighth = samples // 8
    bins_a = np.arange(0, half, 4)
    bins_b = np.arange(2, half, 4)
    bins_o = np.arange(1, half, 2)

    def forward(length, bins):
        phase = (np.arange(length)[:, None] * bins[None, :] % samples) * (2.0 * np.pi / samples)
        return np.cos(phase), -np.sin(phase)

    def inverse(length, bins):
        phase = (bins[:, None] * np.arange(length)[None, :] % samples) * (2.0 * np.pi / samples)
        weight = np.where(bins == 0, 1.0, 2.0)[:, None]
        return weight * np.cos(phase), -weight * np.sin(phase)

    odd_cos, odd_sin = forward(half, bins_o)
    fwd_a = np.concatenate(forward(quarter, bins_a), axis=1)
    fwd_b = np.concatenate(forward(quarter, bins_b), axis=1)
    fwd_o = np.concatenate(
        [odd_cos[:, :eighth], odd_sin[:, :eighth], odd_cos[:, eighth:], odd_sin[:, eighth:]], axis=1
    )
    fwd_even = np.stack([x for t in (fwd_a, fwd_b) for x in split_table(t)])
    fwd_odd = np.stack(split_table(fwd_o))
    inv_cos, inv_sin = inverse(half, bins_o)
    inv_even = np.stack(
        [
            split_table(np.concatenate(inverse(quarter, bins), axis=0))[0]
            for bins in (bins_a, bins_b)
        ]
    )
    inv_odd = np.stack(
        [
            split_table(np.concatenate([inv_cos[rows], inv_sin[rows]], axis=0))[0]
            for rows in (slice(0, eighth), slice(eighth, None))
        ]
    )
    return fwd_even, fwd_odd, inv_even, inv_odd


def dot(left, right):
    return jnp.dot(left, right, preferred_element_type=jnp.float32)


def halves(value):
    high = value.astype(jnp.bfloat16)
    low = (value - high.astype(jnp.float32)).astype(jnp.bfloat16)
    return high, low


def as_column(row):
    n = row.shape[1]
    eye = lax.broadcasted_iota(jnp.int32, (n, n), 0) == lax.broadcasted_iota(jnp.int32, (n, n), 1)
    return jnp.sum(jnp.where(eye, jnp.broadcast_to(row, (n, n)), 0), axis=1, keepdims=True)


def kernel(
    dims,
    traces_hbm,
    needed_hbm,
    home_hbm,
    partner_hbm,
    live_ref,
    fwd_even_hbm,
    fwd_odd_hbm,
    inv_even_hbm,
    inv_odd_hbm,
    out_ref,
    needed_ref,
    home_ref,
    partner_ref,
    traces,
    fwd_even,
    fwd_odd,
    inv_even,
    inv_odd,
    listed_out,
    listed_in,
    terms,
    terms_out,
    terms_in,
    load_sem,
    list_send,
    list_recv,
    term_send,
    term_recv,
):
    groups, win_count, chan_dev, win_dev, samples, listing, cap, cap_rows, blocks, homes, partners = dims
    chips = win_count // 2
    pairs = blocks * homes * partners
    share_rows = pairs // win_count
    pad_rows = terms.shape[2]
    quarter, half, eighth = samples // 4, samples // 2, samples // 8
    group = lax.axis_index("chan")
    win = lax.axis_index("win")
    chip, core = win // 2, win % 2

    loads = [
        pltpu.make_async_copy(src, dst, load_sem.at[i])
        for i, (src, dst) in enumerate(
            (
                (traces_hbm, traces),
                (fwd_even_hbm, fwd_even),
                (fwd_odd_hbm, fwd_odd),
                (inv_even_hbm, inv_even),
                (inv_odd_hbm, inv_odd),
                (needed_hbm, needed_ref),
                (home_hbm, home_ref),
                (partner_hbm, partner_ref),
            )
        )
    ]
    for i in (5, 0, 1, 2, 6, 7):
        loads[i].start()

    barrier = pltpu.get_barrier_semaphore()
    cores = (core, 1 - core)

    def flipped(place, d, count):
        total = 0
        for t in range(count.bit_length() - 1):
            bit = (place // 2**t) % 2
            total = total + (1 - bit if (d >> t) % 2 else bit) * 2**t
        return total

    list_peers = [(d, s) for d in reversed(range(groups)) for s in range(2) if d or s]
    term_peers = [(d, s) for d in reversed(range(chips)) for s in range(2) if d or s]

    def list_id(d, s):
        return {"chan": flipped(group, d, groups), "win": chip * 2 + cores[s]}

    def term_index(d, s):
        return flipped(chip, d, chips) * 2 + cores[s]

    greeted = [list_id(d, s) for d, s in list_peers]
    greeted += [{"win": term_index(d, s)} for d, s in term_peers if d]
    for peer in greeted:
        pl.semaphore_signal(barrier, inc=1, device_id=peer, device_id_type=MESH)

    def bins_along(shape, axis):
        spot = lax.broadcasted_iota(jnp.int32, shape, axis)
        odd_or_b = jnp.where(spot < quarter, (spot - eighth) * 4 + 2, (spot - quarter) * 2 + 1)
        return jnp.where(spot < eighth, spot * 4, odd_or_b)

    bins = bins_along((1, half), 1)
    apart = jnp.abs(bins_along((half, 1), 0) - bins)
    band = jnp.where(apart <= BAND_REACH, 1.0, 0.0).astype(jnp.bfloat16)

    lanes = win_dev * chan_dev
    lane = lax.broadcasted_iota(jnp.int32, (1, lanes), 1)
    lane_win = sum([(lane >= w * chan_dev).astype(jnp.int32) for w in range(1, win_dev)])
    lane_chan = lane - lane_win * chan_dev
    first_mine = group * chan_dev
    place = lax.broadcasted_iota(jnp.int32, (listing, lanes), 0)
    out_row = lax.broadcasted_iota(jnp.int32, (cap_rows, lanes), 0)
    loads[5].wait()
    choose = []
    for d in range(groups):
        owner = flipped(group, d, groups)
        column = as_column(needed_ref[pl.ds(owner, 1), :])
        hit = column == (lane_chan + first_mine)
        found = jnp.sum(jnp.where(hit, place + 1, 0), axis=0, keepdims=True)
        begin = jnp.sum((column < first_mine).astype(jnp.int32), axis=0, keepdims=True)
        target = jnp.where(found > 0, found - 1 - begin + lane_win * cap, -1)
        choose.append(jnp.where(out_row == target, 1.0, 0.0))
    choose = jnp.concatenate(choose, axis=0).astype(jnp.bfloat16)

    loads[0].wait()
    tiles = samples // 128
    rows = jnp.concatenate(
        [
            jnp.concatenate(
                [
                    traces[pl.ds(t * win_dev + w, chan_dev, stride=tiles * win_dev), :]
                    for t in range(tiles)
                ],
                axis=1,
            )
            for w in range(win_dev)
        ],
        axis=0,
    )
    count = rows.shape[0]
    folded = rows[:, :half] + rows[:, half:]
    odd_in = rows[:, :half] - rows[:, half:]
    even_in = (folded[:, :quarter] + folded[:, quarter:], folded[:, :quarter] - folded[:, quarter:])

    def transform(value, high_table, low_table):
        high, low = halves(value)
        both = dot(jnp.concatenate([high, low], axis=0), high_table)
        return both[:count] + both[count:] + dot(high, low_table)

    loads[1].wait()
    spectra = [
        transform(even_in[0], fwd_even[0], fwd_even[1]),
        transform(even_in[1], fwd_even[2], fwd_even[3]),
    ]
    loads[2].wait()
    odd_out = transform(odd_in, fwd_odd[0], fwd_odd[1])
    spectra += [odd_out[:, :quarter], odd_out[:, quarter:]]
    power = jnp.concatenate([s[:, :eighth] ** 2 + s[:, eighth:] ** 2 for s in spectra], axis=1)
    both = dot(jnp.concatenate(halves(power), axis=0), band)
    members = jnp.minimum(bins + BAND_REACH, half - 1) - jnp.maximum(bins - BAND_REACH, 0) + 1
    smooth = (both[:count] + both[count:]) * (1.0 / members.astype(jnp.float32))
    factor = lax.rsqrt(smooth + 1e-05)

    pl.semaphore_wait(barrier, len(greeted))

    list_copies = []
    for h in range(2):
        for k in (h, 2 + h):
            scale = factor[:, k * eighth : (k + 1) * eighth]
            whitened = jnp.concatenate(
                [spectra[k][:, :eighth] * scale, spectra[k][:, eighth:] * scale], axis=1
            ).astype(jnp.bfloat16)
            chosen = dot(choose, whitened).astype(jnp.bfloat16)
            for d in range(groups):
                listed_out[k, d] = chosen[d * cap_rows : (d + 1) * cap_rows]
        copies = []
        for n, (d, s) in enumerate(list_peers):
            copies.append(
                pltpu.make_async_remote_copy(
                    src_ref=listed_out.at[cores[s] * 2 + h, d],
                    dst_ref=listed_in.at[h, s, d],
                    send_sem=list_send.at[h, n],
                    recv_sem=list_recv.at[h, n],
                    device_id=list_id(d, s),
                    device_id_type=MESH,
                )
            )
            copies[-1].start()
        list_copies.append(copies)
        listed_in[h, 0, 0] = listed_out[core * 2 + h, 0]
    for i in (3, 4):
        loads[i].start()
    for i in (6, 7):
        loads[i].wait()

    mine = needed_ref[pl.ds(group, 1), :]
    arrived = lax.broadcasted_iota(jnp.int32, (1, groups * cap_rows), 1)
    code = jnp.full((1, groups * cap_rows), -1, jnp.int32)
    for d in range(groups):
        source = flipped(group, d, groups)
        begin = jnp.sum(
            (mine < source * chan_dev).astype(jnp.int32), axis=1, keepdims=True
        )
        for w in range(win_dev):
            low = d * cap_rows + w * cap
            within = (arrived >= low) & (arrived < low + cap)
            code = jnp.where(within, arrived - low + begin + w * listing, code)
    wanted = [as_column(partner_ref[b : b + 1, :]) for b in range(blocks)]
    wanted += [as_column(home_ref[b : b + 1, :]) for b in range(blocks)]
    wanted = jnp.concatenate(wanted, axis=0)
    per_win = blocks * (homes + partners)
    wanted = jnp.concatenate([wanted + w * listing for w in range(win_dev)], axis=0)
    pick = jnp.where(wanted == code, 1.0, 0.0).astype(jnp.bfloat16)

    term_copies = []
    piece = min(partners, share_rows)
    for h in range(2):
        for copy in list_copies[h]:
            copy.wait_recv()
        tables = [dot(pick, listed_in[h, s].reshape(groups * cap_rows, quarter)) for s in range(2)]
        for b in range(blocks):
            for i in range(homes):
                real = imag = None
                for table in tables:
                    for w in range(win_dev):
                        at = w * per_win + blocks * partners + b * homes + i
                        home_re = table[at : at + 1, :eighth]
                        home_im = table[at : at + 1, eighth:]
                        at = w * per_win + b * partners
                        part_re = table[at : at + partners, :eighth]
                        part_im = table[at : at + partners, eighth:]
                        add_re = home_re * part_re + home_im * part_im
                        add_im = home_im * part_re - home_re * part_im
                        real = add_re if real is None else real + add_re
                        imag = add_im if imag is None else imag + add_im
                term = jnp.concatenate([real, imag], axis=1)
                for j in range(0, partners, piece):
                    row = (b * homes + i) * partners + j
                    owner, inner = row // share_rows, row % share_rows
                    terms[h, owner, inner : inner + piece, :] = term[j : j + piece]
                    terms_out[h, owner, inner : inner + piece, :] = term[j : j + piece].astype(
                        jnp.bfloat16
                    )
        copies = []
        for n, (d, s) in enumerate(term_peers):
            copies.append(
                pltpu.make_async_remote_copy(
                    src_ref=terms_out.at[h, term_index(d, s)],
                    dst_ref=terms_in.at[h, n],
                    send_sem=term_send.at[h, n],
                    recv_sem=term_recv.at[h, n],
                    device_id={"win": term_index(d, s)},
                    device_id_type=MESH,
                )
            )
            copies[-1].start()
        term_copies.append(copies)

    loads[3].wait()
    loads[4].wait()
    for copies in list_copies:
        for copy in copies:
            copy.wait_send()
    parts = [None] * 4
    for h in range(2):
        total = [terms[h, win], None]
        for n, (d, s) in enumerate(term_peers):
            term_copies[h][n].wait_recv()
            arrival = terms_in[h, n].astype(jnp.float32)
            total[s] = arrival if total[s] is None else total[s] + arrival
        for k, value in (
            (h, jnp.where(core == 0, total[0], total[1])),
            (2 + h, jnp.where(core == 0, total[1], total[0])),
        ):
            table = inv_even[h] if k < 2 else inv_odd[h]
            both = dot(jnp.concatenate(halves(value), axis=0), table)
            parts[k] = both[:pad_rows] + both[pad_rows:]
    for copies in term_copies:
        for copy in copies:
            copy.wait_send()
    even = jnp.concatenate([parts[0] + parts[1], parts[0] - parts[1]], axis=1)
    odd = parts[2] + parts[3]
    norm = 1.0 / math.sqrt(samples * win_dev * win_count)
    row = win * share_rows + lax.broadcasted_iota(jnp.int32, (pad_rows, 1), 0)
    norm = jnp.where(row < live_ref[0] * (homes * partners), norm, 0.0)
    out_ref[:, :half] = ((even - odd) * norm)[:share_rows]
    out_ref[:, half:] = ((even + odd) * norm)[:share_rows]


def body(traces, needed, home_slot, partner_slot, live_blocks):
    chan_dev, win_dev, samples = traces.shape
    groups, win_count = lax.axis_size("chan"), lax.axis_size("win")
    listing = needed.shape[1]
    cap = 2 * listing // groups
    cap_rows = -(-win_dev * cap // 16) * 16
    blocks, homes = home_slot.shape
    partners = partner_slot.shape[1]
    share_rows = blocks * homes * partners // win_count
    pad_rows = max(share_rows, 16)
    quarter = samples // 4
    fwd_even, fwd_odd, inv_even, inv_odd = tables(samples)
    dims = (groups, win_count, chan_dev, win_dev, samples, listing, cap, cap_rows, blocks, homes, partners)
    tiled = traces.reshape(chan_dev, win_dev, samples // 128, 128).transpose(0, 2, 1, 3)
    tiled = tiled.reshape(-1, 128)
    vmem = pl.BlockSpec(memory_space=pltpu.VMEM)
    smem = pl.BlockSpec(memory_space=pltpu.SMEM)
    hbm = pl.BlockSpec(memory_space=pltpu.HBM)
    bf16, f32 = jnp.bfloat16, jnp.float32
    return pl.pallas_call(
        functools.partial(kernel, dims),
        out_shape=jax.ShapeDtypeStruct((share_rows, samples), f32),
        in_specs=[hbm] * 4 + [smem] + [hbm] * 4,
        out_specs=vmem,
        scratch_shapes=[
            pltpu.VMEM(needed.shape, jnp.int32),
            pltpu.VMEM(home_slot.shape, jnp.int32),
            pltpu.VMEM(partner_slot.shape, jnp.int32),
            pltpu.VMEM(tiled.shape, f32),
            pltpu.VMEM(fwd_even.shape, bf16),
            pltpu.VMEM(fwd_odd.shape, bf16),
            pltpu.VMEM(inv_even.shape, bf16),
            pltpu.VMEM(inv_odd.shape, bf16),
            pltpu.VMEM((4, groups, cap_rows, quarter), bf16),
            pltpu.VMEM((2, 2, groups, cap_rows, quarter), bf16),
            pltpu.VMEM((2, win_count, pad_rows, quarter), f32),
            pltpu.VMEM((2, win_count, pad_rows, quarter), bf16),
            pltpu.VMEM((2, win_count - 1, pad_rows, quarter), bf16),
            pltpu.SemaphoreType.DMA((8,)),
            pltpu.SemaphoreType.DMA((2, 2 * groups - 1)),
            pltpu.SemaphoreType.DMA((2, 2 * groups - 1)),
            pltpu.SemaphoreType.DMA((2, win_count - 1)),
            pltpu.SemaphoreType.DMA((2, win_count - 1)),
        ],
        compiler_params=pltpu.CompilerParams(
            collective_id=0, has_side_effects=True, vmem_limit_bytes=64 * 1024 * 1024
        ),
        cost_estimate=pl.CostEstimate(
            flops=2_000_000_000, bytes_accessed=4_000_000, transcendentals=100_000
        ),
        name="whiten_cross_stack",
    )(
        tiled,
        needed,
        home_slot,
        partner_slot,
        live_blocks,
        jnp.asarray(fwd_even),
        jnp.asarray(fwd_odd),
        jnp.asarray(inv_even),
        jnp.asarray(inv_odd),
    )


def solution(mesh):
    placed = (P("chan", "win", None), P(), P("chan", None), P("chan", None), P("chan"))
    return jax.shard_map(
        body, mesh=mesh, in_specs=placed, out_specs=P(("chan", "win"), None), check_vma=False
    )
```
